32 devices in a mesh: group: 2 (over y), ctx: 8 (over z, x), tp: 2 (over core).
Axes of the slice: x: 2, y: 2, z: 4, core: 2. Of those that a mesh axis runs over, the one named last changes fastest.
Arguments:
- queries: bfloat16 [4096, 4096], P(('group', 'ctx', 'tp')), parts along dimension 0, may hold values from -100 to 100
- keys: bfloat16 [4096, 2048], P(('group', 'ctx', 'tp')), parts along dimension 0, may hold values from -6 to 6
- values: bfloat16 [4096, 2048], P(('group', 'ctx', 'tp')), parts along dimension 0, may hold values from -6 to 6
- output_gradient: bfloat16 [4096, 4096], P(('group', 'ctx', 'tp')), parts along dimension 0, may hold values from -6 to 6
Outputs:
- attended: bfloat16 [4096, 4096], P(('group', 'ctx', 'tp')), parts along dimension 0
- query_grad: bfloat16 [4096, 4096], P(('group', 'ctx', 'tp')), parts along dimension 0
- key_gradient: bfloat16 [4096, 2048], P(('group', 'ctx', 'tp')), parts along dimension 0
- value_gradient: bfloat16 [4096, 2048], P(('group', 'ctx', 'tp')), parts along dimension 0
The draws below stay inside these ranges and needn't reach their ends.
There are 2 independent parts, one for each index of `group`. The reference program is written for one: setup_inputs(seed, part) draws one part's arguments, and reference() takes and returns one part's arrays. A program takes and returns all parts, laid end to end along the dimension named above; each array names one. Nothing has to cross between parts.
All inputs are finite; a program needn't handle non-finite values.
Results may differ from the reference program's by a relative error of at most 0.02.
Values may be sent and summed in bfloat16 or wider, within the bound.
No kernel may reach another device: no remote copies, remote signals or barrier semaphores. Data moves between devices by JAX's collectives and lax.ppermute only.
A program may use at most 64 MiB of HBM per device.

```python
import math
import jax
import jax.numpy as jnp
from jax import lax

QUERY_HEADS = 32
KEY_VALUE_HEADS = 16
HEAD_SIZE = 128
WINDOW_TOKENS = 1024
TOK_DEV = 256
SEQUENCE_TOKENS = 2048


def draw_queries(key, part):
    key = jax.random.fold_in(key, 17)
    base_key, pick_key, scale_key = jax.random.split(key, 3)
    shape_heads = (SEQUENCE_TOKENS, QUERY_HEADS, HEAD_SIZE)
    base = jnp.clip(jax.random.normal(base_key, shape_heads, jnp.float32), -5.0, 5.0)
    chosen = jax.random.uniform(pick_key, (SEQUENCE_TOKENS, QUERY_HEADS, 1), jnp.float32) < 0.0625
    loud = jnp.exp(jax.random.uniform(scale_key, (SEQUENCE_TOKENS, QUERY_HEADS, 1), jnp.float32, math.log(6.0), math.log(20.0)))
    quiet = 2.5
    row_scale = jnp.where(chosen, loud, quiet)
    return (base * row_scale).reshape(SEQUENCE_TOKENS, QUERY_HEADS * HEAD_SIZE).astype(jnp.bfloat16)


def shard_levels(own_key, dims, pieces, least, largest):
    gain = 1.0
    for dim, blocks in pieces:
        heights = jax.random.uniform(jax.random.fold_in(jax.random.fold_in(own_key, 6), dim), (blocks,), jnp.float32, least / len(pieces), largest / len(pieces))
        gain = gain * jnp.repeat(jnp.exp(heights), dims[dim] // blocks).reshape((-1,) + (1,) * (len(dims) - 1 - dim))
    return gain


def centred(rng, shape, deviation, bound, cuts=(), kind=jnp.bfloat16):
    result = jax.random.normal(rng, shape, jnp.float32) * deviation
    if len(cuts) > 0:
        result = shard_levels(rng, shape, cuts, -0.22, 0.18) * result
    return jnp.clip(result, min=-bound, max=bound).astype(kind)


def setup_inputs(seed: int = 0, part: int = 0) -> dict:
    streams_of = jax.random.split(jax.random.key(seed), 5)
    part_keys = jax.random.split(jax.random.fold_in(streams_of[4], part), 5)
    queries = draw_queries(jax.random.fold_in(jax.random.fold_in(streams_of[4], part), 71), part)
    keys = centred(part_keys[1], (SEQUENCE_TOKENS, KEY_VALUE_HEADS * HEAD_SIZE), 1.0, 6.0, ((0, 16),))
    values = centred(part_keys[2], (SEQUENCE_TOKENS, KEY_VALUE_HEADS * HEAD_SIZE), 1.0, 6.0, ((0, 16),))
    output_gradient = centred(part_keys[3], (SEQUENCE_TOKENS, QUERY_HEADS * HEAD_SIZE), 1.0, 6.0, ((0, 16),))
    return dict(queries=queries, keys=keys, values=values, output_gradient=output_gradient)


score_scale = 1.0 / 12.0
softcap_value = 50.0
highest = lax.Precision.HIGHEST


def reference(queries, keys, values, output_gradient):
    query_group_size = QUERY_HEADS // KEY_VALUE_HEADS
    blocks_total = SEQUENCE_TOKENS // TOK_DEV
    span_keys = WINDOW_TOKENS + TOK_DEV
    heads_of_queries = queries.reshape(SEQUENCE_TOKENS, KEY_VALUE_HEADS, query_group_size, HEAD_SIZE).transpose(1, 2, 0, 3)
    gradient_heads = output_gradient.reshape(SEQUENCE_TOKENS, KEY_VALUE_HEADS, query_group_size, HEAD_SIZE).transpose(1, 2, 0, 3)
    padding_rows = jnp.zeros((KEY_VALUE_HEADS, WINDOW_TOKENS, HEAD_SIZE), jnp.bfloat16)
    heads_of_keys = jnp.concatenate([padding_rows, keys.reshape(SEQUENCE_TOKENS, KEY_VALUE_HEADS, HEAD_SIZE).transpose(1, 0, 2)], axis=1)
    heads_of_values = jnp.concatenate([padding_rows, values.reshape(SEQUENCE_TOKENS, KEY_VALUE_HEADS, HEAD_SIZE).transpose(1, 0, 2)], axis=1)

    def one_block(carried, block_index):
        key_gradient_total, value_gradient_total = carried
        first_row = (block_index * TOK_DEV).astype(jnp.int32)
        query_blk = lax.dynamic_slice_in_dim(heads_of_queries, first_row, TOK_DEV, 2).astype(jnp.float32)
        grad_blk = lax.dynamic_slice_in_dim(gradient_heads, first_row, TOK_DEV, 2).astype(jnp.float32)
        key_blk = lax.dynamic_slice_in_dim(heads_of_keys, first_row, span_keys, 1).astype(jnp.float32)
        value_blk = lax.dynamic_slice_in_dim(heads_of_values, first_row, span_keys, 1).astype(jnp.float32)
        query_pos = first_row + jnp.arange(TOK_DEV, dtype=jnp.int32)
        key_pos = first_row - WINDOW_TOKENS + jnp.arange(span_keys, dtype=jnp.int32)
        allowed = (key_pos[None, :] <= query_pos[:, None]) & (key_pos[None, :] > query_pos[:, None] - WINDOW_TOKENS) & (key_pos[None, :] >= 0)
        score = jnp.einsum('hgqd,hkd->hgqk', query_blk, key_blk, precision=highest) * score_scale
        capped = softcap_value * jnp.tanh(score / softcap_value)
        expo = jnp.where(allowed, jnp.exp(capped), jnp.float32(0.0))
        normalizer = jnp.sum(expo, axis=-1, keepdims=True)
        weights = expo / normalizer
        probs = weights.astype(jnp.bfloat16)
        probs = lax.optimization_barrier(probs)
        attended_blk = jnp.einsum('hgqk,hkd->hgqd', probs.astype(jnp.float32), value_blk, precision=highest).astype(jnp.bfloat16)
        attended_blk = lax.optimization_barrier(attended_blk)
        grad_dot = jnp.sum(grad_blk * attended_blk.astype(jnp.float32), axis=-1, keepdims=True)
        dprob = jnp.einsum('hgqd,hkd->hgqk', grad_blk, value_blk, precision=highest)
        dscore = (weights * (dprob - grad_dot) * (1.0 - (capped / softcap_value) ** 2) * score_scale).astype(jnp.bfloat16)
        dscore = lax.optimization_barrier(dscore).astype(jnp.float32)
        query_grad_blk = jnp.einsum('hgqk,hkd->hgqd', dscore, key_blk, precision=highest).astype(jnp.bfloat16)
        key_part = jnp.einsum('hgqk,hgqd->hkd', dscore, query_blk, precision=highest)
        value_part = jnp.einsum('hgqk,hgqd->hkd', probs.astype(jnp.float32), grad_blk, precision=highest)
        key_gradient_total = lax.dynamic_update_slice_in_dim(key_gradient_total, lax.dynamic_slice_in_dim(key_gradient_total, first_row, span_keys, 1) + key_part, first_row, 1)
        value_gradient_total = lax.dynamic_update_slice_in_dim(value_gradient_total, lax.dynamic_slice_in_dim(value_gradient_total, first_row, span_keys, 1) + value_part, first_row, 1)
        return (key_gradient_total, value_gradient_total), (attended_blk, query_grad_blk)

    zero_gradient_total = jnp.zeros((KEY_VALUE_HEADS, WINDOW_TOKENS + SEQUENCE_TOKENS, HEAD_SIZE), jnp.float32)
    (key_gradient_total, value_gradient_total), (attended_all, query_grad_all) = lax.scan(one_block, (zero_gradient_total, zero_gradient_total), jnp.arange(blocks_total, dtype=jnp.int32))
    attended = attended_all.transpose(0, 3, 1, 2, 4).reshape(SEQUENCE_TOKENS, QUERY_HEADS * HEAD_SIZE)
    query_grad = query_grad_all.transpose(0, 3, 1, 2, 4).reshape(SEQUENCE_TOKENS, QUERY_HEADS * HEAD_SIZE)
    key_gradient = key_gradient_total[:, WINDOW_TOKENS:].transpose(1, 0, 2).reshape(SEQUENCE_TOKENS, KEY_VALUE_HEADS * HEAD_SIZE).astype(jnp.bfloat16)
    value_gradient = value_gradient_total[:, WINDOW_TOKENS:].transpose(1, 0, 2).reshape(SEQUENCE_TOKENS, KEY_VALUE_HEADS * HEAD_SIZE).astype(jnp.bfloat16)
    return (attended, query_grad, key_gradient, value_gradient)
```

```python
import functools
import math

import jax
import jax.numpy as jnp
from jax import lax
from jax.experimental import pallas as pl
from jax.experimental.pallas import tpu as pltpu
from jax.sharding import PartitionSpec as P

HEAD = 128
WINDOW = 1024
INNER = 2
CHUNKS = (2, 2)
SOFTCAP = 50.0
TANH_SCALE = 1.0 / (12.0 * SOFTCAP)
EXP2_SCALE = SOFTCAP * math.log2(math.e)
SCORE_SCALE = 1.0 / 12.0
F32 = jnp.float32
BF16 = jnp.bfloat16


def dot(a, b, ca, cb):
    return lax.dot_general(a, b, (((ca,), (cb,)), ((), ())), preferred_element_type=F32)


def vmem():
    return pl.BlockSpec(memory_space=pltpu.VMEM)


def smem():
    return pl.BlockSpec(memory_space=pltpu.SMEM)


def head_cols(index):
    return pl.ds(pl.multiple_of(index * HEAD, HEAD), HEAD)


def pack_kernel(chunks, members, group, heads_dev, info, a_ref, b_ref, *outs):
    me = info[0]
    first = 0
    for c, heads in enumerate(chunks):
        for m in range(members):
            out = outs[c * members + m]
            base = (me ^ m) * heads_dev + first
            for h in range(heads):
                for g in range(group):
                    source = head_cols((base + h) * group + g)
                    out[:, (2 * h * group + g) * HEAD : (2 * h * group + g + 1) * HEAD] = a_ref[:, source]
                    out[:, ((2 * h + 1) * group + g) * HEAD : ((2 * h + 1) * group + g + 1) * HEAD] = b_ref[:, source]
        first += heads


def pack(info, a, b, chunks, members, group, heads_dev):
    rows = a.shape[0]
    return pl.pallas_call(
        functools.partial(pack_kernel, chunks, members, group, heads_dev),
        out_shape=[
            jax.ShapeDtypeStruct((rows, 2 * h * group * HEAD), BF16) for h in chunks for _ in range(members)
        ],
        in_specs=[smem(), vmem(), vmem()],
        out_specs=[vmem()] * (len(chunks) * members),
        compiler_params=pltpu.CompilerParams(vmem_limit_bytes=40 * 2**20),
        name="pack",
    )(info, a, b)


def unpack_kernel(chunks, members, group, heads_dev, info, *refs):
    me = info[0]
    ins, (a_ref, b_ref) = refs[:-2], refs[-2:]
    first = 0
    for c, heads in enumerate(chunks):
        for m in range(members):
            src = ins[c * members + m]
            base = (me ^ m) * heads_dev + first
            for h in range(heads):
                for g in range(group):
                    target = head_cols((base + h) * group + g)
                    a_ref[:, target] = src[:, (2 * h * group + g) * HEAD : (2 * h * group + g + 1) * HEAD]
                    b_ref[:, target] = src[:, ((2 * h + 1) * group + g) * HEAD : ((2 * h + 1) * group + g + 1) * HEAD]
        first += heads


def unpack(info, pieces, chunks, members, group, heads_dev):
    rows = pieces[0].shape[0]
    width = members * heads_dev * group * HEAD
    return pl.pallas_call(
        functools.partial(unpack_kernel, chunks, members, group, heads_dev),
        out_shape=[jax.ShapeDtypeStruct((rows, width), BF16)] * 2,
        in_specs=[smem()] + [vmem()] * len(pieces),
        out_specs=[vmem()] * 2,
        compiler_params=pltpu.CompilerParams(vmem_limit_bytes=40 * 2**20),
        name="unpack",
    )(info, *pieces)


def attention_kernel(members, hops, group, rows, info, *refs):
    planes = hops + 1
    kv_refs = refs[:planes]
    q_refs = refs[planes : planes + members]
    o_refs = refs[planes + members : planes + 2 * members]
    dkv_refs = refs[planes + 2 * members : 2 * planes + 2 * members]
    k_s, v_s, kt_s, vt_s, dk_s, dv_s, p_s, eg_s, ds_s = refs[2 * planes + 2 * members :]
    me = info[0]
    plane = info[1]
    blocks = WINDOW // rows + 1
    wide = group * rows
    span = blocks * rows
    for k in range(planes):
        for s in range(members):
            at = (k * members + s) * rows
            piece = kv_refs[k][me ^ s]
            k_s[at : at + rows, :] = piece[:, :HEAD]
            v_s[at : at + rows, :] = piece[:, HEAD:]
            kt_s[:, at : at + rows] = piece[:, :HEAD].T
            vt_s[:, at : at + rows] = piece[:, HEAD:].T
    dk_s[...] = jnp.zeros_like(dk_s)
    dv_s[...] = jnp.zeros_like(dv_s)
    key_at = lax.broadcasted_iota(jnp.int32, (rows, wide), 0)
    query_at = lax.broadcasted_iota(jnp.int32, (rows, wide), 1) % rows
    after = key_at > query_at
    for m in range(members):
        s = me ^ m
        base = pl.multiple_of(s * rows, rows)
        q_all = q_refs[m]
        q = jnp.concatenate([q_all[:, g * HEAD : (g + 1) * HEAD] for g in range(group)], axis=0)
        go = jnp.concatenate([q_all[:, (group + g) * HEAD : (group + g + 1) * HEAD] for g in range(group)], axis=0)
        total = jnp.zeros((1, wide), F32)
        for b in range(blocks):
            score = dot(k_s[pl.ds(pl.multiple_of(base + b * rows, rows), rows), :], q, 1, 1)
            t = jnp.tanh(score * TANH_SCALE)
            e = jnp.exp2(t * EXP2_SCALE)
            if b == 0:
                e = jnp.where(after, e, 0.0)
            if b == blocks - 1:
                e = jnp.where(after, 0.0, e)
            seen = plane - hops + lax.div(s + b, members) >= 0
            total = total + jnp.where(seen, jnp.sum(e, axis=0, keepdims=True), 0.0)
            p_s[b * rows : (b + 1) * rows, :] = e.astype(BF16)
            eg_s[b * rows : (b + 1) * rows, :] = e * (1.0 - t * t)
        inverse = 1.0 / total
        band = pl.ds(base, span)
        p = p_s[...]
        ot = (dot(vt_s[:, band], p, 1, 0) * inverse).astype(BF16)
        got = (go.astype(F32).T * inverse).astype(BF16)
        gdot = jnp.sum(ot.astype(F32) * got.astype(F32), axis=0, keepdims=True)
        for b in range(blocks):
            part = slice(b * rows, (b + 1) * rows)
            dp = dot(v_s[pl.ds(pl.multiple_of(base + b * rows, rows), rows), :], got, 1, 0)
            ds_s[part, :] = ((dp - gdot) * eg_s[part, :]).astype(BF16)
        ds = ds_s[...]
        dqt = dot(kt_s[:, band], ds, 1, 0) * SCORE_SCALE
        dk_s[band, :] += dot(ds, q, 1, 0)
        dv_s[band, :] += dot(p, got, 1, 1)
        o = ot.astype(F32).T.astype(BF16)
        dq = dqt.T.astype(BF16)
        for g in range(group):
            o_refs[m][:, g * HEAD : (g + 1) * HEAD] = o[g * rows : (g + 1) * rows]
            o_refs[m][:, (group + g) * HEAD : (group + g + 1) * HEAD] = dq[g * rows : (g + 1) * rows]
    for k in range(planes):
        for s in range(members):
            at = (k * members + s) * rows
            dkv_refs[k][me ^ s, :, :HEAD] = (dk_s[at : at + rows, :] * SCORE_SCALE).astype(BF16)
            dkv_refs[k][me ^ s, :, HEAD:] = dv_s[at : at + rows, :].astype(BF16)


def attention(info, kvs, qs, group):
    planes, members = len(kvs), len(qs)
    rows = qs[0].shape[0]
    heads = kvs[0].shape[2] // (2 * HEAD)
    keys_all = planes * members * rows
    wide = group * rows
    span = WINDOW + rows
    kv_spec = pl.BlockSpec((members, rows, 2 * HEAD), lambda h: (0, 0, h))
    q_spec = pl.BlockSpec((rows, 2 * group * HEAD), lambda h: (0, h))
    return pl.pallas_call(
        functools.partial(attention_kernel, members, planes - 1, group, rows),
        grid=(heads,),
        out_shape=[jax.ShapeDtypeStruct(q.shape, BF16) for q in qs]
        + [jax.ShapeDtypeStruct(kv.shape, BF16) for kv in kvs],
        in_specs=[smem()] + [kv_spec] * planes + [q_spec] * members,
        out_specs=[q_spec] * members + [kv_spec] * planes,
        scratch_shapes=[
            pltpu.VMEM((keys_all, HEAD), BF16),
            pltpu.VMEM((keys_all, HEAD), BF16),
            pltpu.VMEM((HEAD, keys_all), BF16),
            pltpu.VMEM((HEAD, keys_all), BF16),
            pltpu.VMEM((keys_all, HEAD), F32),
            pltpu.VMEM((keys_all, HEAD), F32),
            pltpu.VMEM((span, wide), BF16),
            pltpu.VMEM((span, wide), F32),
            pltpu.VMEM((span, wide), BF16),
        ],
        compiler_params=pltpu.CompilerParams(vmem_limit_bytes=40 * 2**20),
        cost_estimate=pl.CostEstimate(
            flops=12 * heads * members * wide * span * HEAD,
            bytes_accessed=2 * (2 * planes * kvs[0].size + 2 * members * qs[0].size),
            transcendentals=2 * heads * members * wide * span,
        ),
        name="attention",
    )(info, *kvs, *qs)


def on_device(queries, keys, values, output_gradient):
    rows = queries.shape[0]
    tp = lax.axis_size("tp")
    ctx = lax.axis_size("ctx")
    members = INNER * tp
    planes = ctx // INNER
    heads_dev = keys.shape[1] // HEAD // members
    group = queries.shape[1] // keys.shape[1]
    hops = max(1, WINDOW // (members * rows))
    device = lax.axis_index("ctx") * tp + lax.axis_index("tp")
    me = device % members
    plane = device // members
    info = jnp.stack([me, plane]).astype(jnp.int32)
    axes = ("ctx", "tp")

    def swap(piece, m):
        if m == 0:
            return piece
        return lax.ppermute(piece, axes, [(i, i ^ m) for i in range(ctx * tp)])

    def hop(array, by):
        pairs = [(i, i + by * members) for i in range(ctx * tp) if 0 <= i + by * members < ctx * tp]
        return lax.ppermute(array, axes, pairs)

    kv_packed = pack(info, keys, values, CHUNKS, members, 1, heads_dev)
    q_packed = pack(info, queries, output_gradient, CHUNKS, members, group, heads_dev)
    kv_own = []
    for c in range(len(CHUNKS)):
        kv_own.append(jnp.stack([swap(kv_packed[c * members + m], m) for m in range(members)]))
    q_pieces = []
    kv_all = []
    for c in range(len(CHUNKS)):
        halo = [kv_own[c]]
        for _ in range(hops):
            halo.insert(0, hop(halo[0], 1))
        kv_all.append(halo)
        q_pieces.append([swap(q_packed[c * members + m], m) for m in range(members)])
    o_pieces, dkv_pieces = [], []
    for c in range(len(CHUNKS)):
        results = attention(info, kv_all[c], q_pieces[c], group)
        os, dkvs = results[:members], results[members:]
        o_pieces += [swap(os[m], m) for m in range(members)]
        carried = dkvs[0]
        for k in range(1, hops + 1):
            carried = (hop(carried, -1).astype(F32) + dkvs[k].astype(F32)).astype(BF16)
        dkv_pieces += [swap(carried[m], m) for m in range(members)]
    attended, query_grad = unpack(info, o_pieces, CHUNKS, members, group, heads_dev)
    key_grad, value_grad = unpack(info, dkv_pieces, CHUNKS, members, 1, heads_dev)
    return attended, query_grad, key_grad, value_grad


def solution(mesh):
    placed = P(("group", "ctx", "tp"), None)
    return jax.shard_map(
        on_device, mesh=mesh, in_specs=(placed,) * 4, out_specs=(placed,) * 4, check_vma=False
    )
```

```python
import functools
import math

import jax
import jax.numpy as jnp
from jax import lax
from jax.experimental import pallas as pl
from jax.experimental.pallas import tpu as pltpu
from jax.sharding import PartitionSpec as P

HEAD = 128
WINDOW = 1024
INNER = 2
CHUNKS = (2, 2)
STEPS = ("kv0", "kv1", "z0", "q0", "q1", "z1", "att0", "o0", "r0", "dx0", "att1", "o1", "r1", "dx1")
GATES = {
    "kv1": ("kv0",),
    "pack": ("kv0",),
    "q1": ("q0",),
    "r11": ("o0",),
    "r21": ("o1",),
    "dx1": ("o1",),
}
SOFTCAP = 50.0
TANH_SCALE = 1.0 / (12.0 * SOFTCAP)
EXP2_SCALE = SOFTCAP * math.log2(math.e)
SCORE_SCALE = 1.0 / 12.0
F32 = jnp.float32
BF16 = jnp.bfloat16


def dot(a, b, ca, cb):
    return lax.dot_general(a, b, (((ca,), (cb,)), ((), ())), preferred_element_type=F32)


def vmem():
    return pl.BlockSpec(memory_space=pltpu.VMEM)


def smem():
    return pl.BlockSpec(memory_space=pltpu.SMEM)


def head_cols(index):
    return pl.ds(pl.multiple_of(index * HEAD, HEAD), HEAD)


def pack_kernel(chunks, members, group, heads_dev, info, a_ref, b_ref, *outs):
    me = info[0]
    first = 0
    for c, heads in enumerate(chunks):
        for m in range(members):
            out = outs[c * members + m]
            base = (me ^ m) * heads_dev + first
            for h in range(heads):
                for g in range(group):
                    source = head_cols((base + h) * group + g)
                    out[:, (2 * h * group + g) * HEAD : (2 * h * group + g + 1) * HEAD] = a_ref[:, source]
                    out[:, ((2 * h + 1) * group + g) * HEAD : ((2 * h + 1) * group + g + 1) * HEAD] = b_ref[:, source]
        first += heads


def pack(info, a, b, chunks, members, group, heads_dev):
    rows = a.shape[0]
    return pl.pallas_call(
        functools.partial(pack_kernel, chunks, members, group, heads_dev),
        out_shape=[
            jax.ShapeDtypeStruct((rows, 2 * h * group * HEAD), BF16) for h in chunks for _ in range(members)
        ],
        in_specs=[smem(), vmem(), vmem()],
        out_specs=[vmem()] * (len(chunks) * members),
        compiler_params=pltpu.CompilerParams(vmem_limit_bytes=40 * 2**20),
        name="pack",
    )(info, a, b)


def unpack_kernel(chunks, members, group, heads_dev, info, *refs):
    me = info[0]
    ins, (a_ref, b_ref) = refs[:-2], refs[-2:]
    first = 0
    for c, heads in enumerate(chunks):
        for m in range(members):
            src = ins[c * members + m]
            base = (me ^ m) * heads_dev + first
            for h in range(heads):
                for g in range(group):
                    target = head_cols((base + h) * group + g)
                    a_ref[:, target] = src[:, (2 * h * group + g) * HEAD : (2 * h * group + g + 1) * HEAD]
                    b_ref[:, target] = src[:, ((2 * h + 1) * group + g) * HEAD : ((2 * h + 1) * group + g + 1) * HEAD]
        first += heads


def unpack(info, pieces, chunks, members, group, heads_dev):
    rows = pieces[0].shape[0]
    width = members * heads_dev * group * HEAD
    return pl.pallas_call(
        functools.partial(unpack_kernel, chunks, members, group, heads_dev),
        out_shape=[jax.ShapeDtypeStruct((rows, width), BF16)] * 2,
        in_specs=[smem()] + [vmem()] * len(pieces),
        out_specs=[vmem()] * 2,
        compiler_params=pltpu.CompilerParams(vmem_limit_bytes=40 * 2**20),
        name="unpack",
    )(info, *pieces)


def attention_kernel(members, hops, group, rows, info, *refs):
    planes = hops + 1
    kv_refs = refs[:planes]
    q_refs = refs[planes : planes + members]
    o_refs = refs[planes + members : planes + 2 * members]
    dkv_refs = refs[planes + 2 * members : 2 * planes + 2 * members]
    k_s, v_s, kt_s, vt_s, dk_s, dv_s, p_s, eg_s, ds_s = refs[2 * planes + 2 * members :]
    me = info[0]
    plane = info[1]
    blocks = WINDOW // rows + 1
    wide = group * rows
    span = blocks * rows
    for k in range(planes):
        for s in range(members):
            at = (k * members + s) * rows
            piece = kv_refs[k][me ^ s]
            k_s[at : at + rows, :] = piece[:, :HEAD]
            v_s[at : at + rows, :] = piece[:, HEAD:]
            kt_s[:, at : at + rows] = piece[:, :HEAD].T
            vt_s[:, at : at + rows] = piece[:, HEAD:].T
    dk_s[...] = jnp.zeros_like(dk_s)
    dv_s[...] = jnp.zeros_like(dv_s)
    key_at = lax.broadcasted_iota(jnp.int32, (rows, wide), 0)
    query_at = lax.broadcasted_iota(jnp.int32, (rows, wide), 1) % rows
    after = key_at > query_at
    for m in range(members):
        s = me ^ m
        base = pl.multiple_of(s * rows, rows)
        q_all = q_refs[m]
        q = jnp.concatenate([q_all[:, g * HEAD : (g + 1) * HEAD] for g in range(group)], axis=0)
        go = jnp.concatenate([q_all[:, (group + g) * HEAD : (group + g + 1) * HEAD] for g in range(group)], axis=0)
        total = jnp.zeros((1, wide), F32)
        for b in range(blocks):
            score = dot(k_s[pl.ds(pl.multiple_of(base + b * rows, rows), rows), :], q, 1, 1)
            t = jnp.tanh(score * TANH_SCALE)
            e = jnp.exp2(t * EXP2_SCALE)
            if b == 0:
                e = jnp.where(after, e, 0.0)
            if b == blocks - 1:
                e = jnp.where(after, 0.0, e)
            seen = plane - hops + lax.div(s + b, members) >= 0
            total = total + jnp.where(seen, jnp.sum(e, axis=0, keepdims=True), 0.0)
            p_s[b * rows : (b + 1) * rows, :] = e.astype(BF16)
            eg_s[b * rows : (b + 1) * rows, :] = e * (1.0 - t * t)
        inverse = 1.0 / total
        band = pl.ds(base, span)
        p = p_s[...]
        ot = (dot(vt_s[:, band], p, 1, 0) * inverse).astype(BF16)
        got = (go.astype(F32).T * inverse).astype(BF16)
        gdot = jnp.sum(ot.astype(F32) * got.astype(F32), axis=0, keepdims=True)
        for b in range(blocks):
            part = slice(b * rows, (b + 1) * rows)
            dp = dot(v_s[pl.ds(pl.multiple_of(base + b * rows, rows), rows), :], got, 1, 0)
            ds_s[part, :] = ((dp - gdot) * eg_s[part, :]).astype(BF16)
        ds = ds_s[...]
        dqt = dot(kt_s[:, band], ds, 1, 0) * SCORE_SCALE
        dk_s[band, :] += dot(ds, q, 1, 0)
        dv_s[band, :] += dot(p, got, 1, 1)
        o = ot.astype(F32).T.astype(BF16)
        dq = dqt.T.astype(BF16)
        for g in range(group):
            o_refs[m][:, g * HEAD : (g + 1) * HEAD] = o[g * rows : (g + 1) * rows]
            o_refs[m][:, (group + g) * HEAD : (group + g + 1) * HEAD] = dq[g * rows : (g + 1) * rows]
    for k in range(planes):
        for s in range(members):
            at = (k * members + s) * rows
            dkv_refs[k][me ^ s, :, :HEAD] = (dk_s[at : at + rows, :] * SCORE_SCALE).astype(BF16)
            dkv_refs[k][me ^ s, :, HEAD:] = dv_s[at : at + rows, :].astype(BF16)


def attention(info, kvs, qs, group):
    planes, members = len(kvs), len(qs)
    rows = qs[0].shape[0]
    heads = kvs[0].shape[2] // (2 * HEAD)
    keys_all = planes * members * rows
    wide = group * rows
    span = WINDOW + rows
    kv_spec = pl.BlockSpec((members, rows, 2 * HEAD), lambda h: (0, 0, h))
    q_spec = pl.BlockSpec((rows, 2 * group * HEAD), lambda h: (0, h))
    return pl.pallas_call(
        functools.partial(attention_kernel, members, planes - 1, group, rows),
        grid=(heads,),
        out_shape=[jax.ShapeDtypeStruct(q.shape, BF16) for q in qs]
        + [jax.ShapeDtypeStruct(kv.shape, BF16) for kv in kvs],
        in_specs=[smem()] + [kv_spec] * planes + [q_spec] * members,
        out_specs=[q_spec] * members + [kv_spec] * planes,
        scratch_shapes=[
            pltpu.VMEM((keys_all, HEAD), BF16),
            pltpu.VMEM((keys_all, HEAD), BF16),
            pltpu.VMEM((HEAD, keys_all), BF16),
            pltpu.VMEM((HEAD, keys_all), BF16),
            pltpu.VMEM((keys_all, HEAD), F32),
            pltpu.VMEM((keys_all, HEAD), F32),
            pltpu.VMEM((span, wide), BF16),
            pltpu.VMEM((span, wide), F32),
            pltpu.VMEM((span, wide), BF16),
        ],
        compiler_params=pltpu.CompilerParams(vmem_limit_bytes=40 * 2**20),
        cost_estimate=pl.CostEstimate(
            flops=12 * heads * members * wide * span * HEAD,
            bytes_accessed=2 * (2 * planes * kvs[0].size + 2 * members * qs[0].size),
            transcendentals=2 * heads * members * wide * span,
        ),
        name="attention",
    )(info, *kvs, *qs)


def after(value, *earlier):
    leaves = [leaf for leaf in jax.tree.leaves(earlier)]
    return lax.optimization_barrier((value, leaves))[0] if leaves else value


def on_device(queries, keys, values, output_gradient):
    rows = queries.shape[0]
    tp = lax.axis_size("tp")
    ctx = lax.axis_size("ctx")
    members = INNER * tp
    heads_dev = keys.shape[1] // HEAD // members
    group = queries.shape[1] // keys.shape[1]
    hops = max(1, WINDOW // (members * rows))
    device = lax.axis_index("ctx") * tp + lax.axis_index("tp")
    info = jnp.stack([device % members, device // members]).astype(jnp.int32)
    axes = ("ctx", "tp")
    count = len(CHUNKS)

    def swap(pieces):
        pairs = [[(i, i ^ m) for i in range(ctx * tp)] for m in range(members)]
        return [pieces[0]] + [lax.ppermute(pieces[m], axes, pairs[m]) for m in range(1, members)]

    def hop(array, by):
        pairs = [(i, i + by * members) for i in range(ctx * tp) if 0 <= i + by * members < ctx * tp]
        return lax.ppermute(array, axes, pairs)

    kv_packed = pack(info, keys, values, CHUNKS, members, 1, heads_dev)
    done = {}
    q_packed = []

    def gated(value, step):
        earlier = [done[name] for name in GATES.get(step, ()) if name in done]
        return after(value, *earlier)

    def run(step):
        kind, c = step[:-1], int(step[-1])
        if kind == "kv":
            done[step] = swap(gated(kv_packed[c * members : (c + 1) * members], step))
        elif kind == "q":
            if not q_packed:
                q_packed.extend(
                    pack(info, gated(queries, "pack"), output_gradient, CHUNKS, members, group, heads_dev)
                )
            done[step] = swap(gated(q_packed[c * members : (c + 1) * members], step))
        elif kind.startswith("z"):
            k = int(kind[1:])
            if k == 1:
                done[f"z0{c}"] = jnp.stack(done[f"kv{c}"])
            done[step] = hop(gated(done[f"z{k - 1}{c}"], step), 1)
        elif kind == "att":
            halo = [done[f"z{k}{c}"] for k in range(hops, -1, -1)]
            halo, pieces = gated((halo, done[f"q{c}"]), step)
            results = attention(info, halo, pieces, group)
            done[step] = results[members:]
            done[f"os{c}"] = results[:members]
            done[f"r0{c}"] = results[members]
        elif kind == "o":
            done[step] = swap(gated(done[f"os{c}"], step))
        elif kind.startswith("r"):
            k = int(kind[1:])
            arrived = hop(gated(done[f"r{k - 1}{c}"], step), -1)
            done[step] = (arrived.astype(F32) + done[f"att{c}"][k].astype(F32)).astype(BF16)
        else:
            carried = gated(done[f"r{hops}{c}"], step)
            done[step] = swap([carried[m] for m in range(members)])

    for step in STEPS:
        kind = step[:-1]
        if kind in ("z", "r"):
            for k in range(1, hops + 1):
                run(f"{kind}{k}{step[-1]}")
        else:
            run(step)
    attended, query_grad = unpack(
        info, sum([done[f"o{c}"] for c in range(count)], []), CHUNKS, members, group, heads_dev
    )
    key_grad, value_grad = unpack(
        info, sum([done[f"dx{c}"] for c in range(count)], []), CHUNKS, members, 1, heads_dev
    )
    return attended, query_grad, key_grad, value_grad


def solution(mesh):
    placed = P(("group", "ctx", "tp"), None)
    return jax.shard_map(
        on_device, mesh=mesh, in_specs=(placed,) * 4, out_specs=(placed,) * 4, check_vma=False
    )
```

```python
import functools
import math

import jax
import jax.numpy as jnp
from jax import lax
from jax.experimental import pallas as pl
from jax.experimental.pallas import tpu as pltpu
from jax.sharding import PartitionSpec as P

HEAD = 128
WINDOW = 1024
INNER = 2
CHUNKS = (2, 2)
CALLS = ((0, 0, 2), (1, 0, 2))
STEPS = ("kv0", "kv1", "z0", "q0", "q1", "z1", "att0", "o0", "r0", "dx0", "att1", "o1", "r1", "dx1")
GATES = {
    "kv1": ("kv0",),
    "pack": ("kv0",),
    "q1": ("q0",),
    "r11": ("o0",),
    "r21": ("o1",),
    "dx1": ("o1",),
}
SOFTCAP = 50.0
TANH_SCALE = 1.0 / (12.0 * SOFTCAP)
EXP2_SCALE = SOFTCAP * math.log2(math.e)
SCORE_SCALE = 1.0 / 12.0
F32 = jnp.float32
BF16 = jnp.bfloat16
BUFFERS = 2
JOIN = 3


def dot(a, b, ca, cb):
    return lax.dot_general(a, b, (((ca,), (cb,)), ((), ())), preferred_element_type=F32)


def vmem():
    return pl.BlockSpec(memory_space=pltpu.VMEM)


def smem():
    return pl.BlockSpec(memory_space=pltpu.SMEM)


def head_cols(index):
    return pl.ds(pl.multiple_of(index * HEAD, HEAD), HEAD)


def pack_kernel(chunks, members, group, heads_dev, info, a_ref, b_ref, *outs):
    me = info[0]
    first = 0
    for c, heads in enumerate(chunks):
        for m in range(members):
            out = outs[c * members + m]
            base = (me ^ m) * heads_dev + first
            for h in range(heads):
                for g in range(group):
                    source = head_cols((base + h) * group + g)
                    out[:, (2 * h * group + g) * HEAD : (2 * h * group + g + 1) * HEAD] = a_ref[:, source]
                    out[:, ((2 * h + 1) * group + g) * HEAD : ((2 * h + 1) * group + g + 1) * HEAD] = b_ref[:, source]
        first += heads


def pack(info, a, b, chunks, members, group, heads_dev):
    rows = a.shape[0]
    return pl.pallas_call(
        functools.partial(pack_kernel, chunks, members, group, heads_dev),
        out_shape=[
            jax.ShapeDtypeStruct((rows, 2 * h * group * HEAD), BF16) for h in chunks for _ in range(members)
        ],
        in_specs=[smem(), vmem(), vmem()],
        out_specs=[vmem()] * (len(chunks) * members),
        compiler_params=pltpu.CompilerParams(vmem_limit_bytes=40 * 2**20),
        name="pack",
    )(info, a, b)


def unpack_kernel(chunks, members, group, heads_dev, info, *refs):
    me = info[0]
    ins, (a_ref, b_ref) = refs[:-2], refs[-2:]
    first = 0
    for c, heads in enumerate(chunks):
        for m in range(members):
            src = ins[c * members + m]
            base = (me ^ m) * heads_dev + first
            for h in range(heads):
                for g in range(group):
                    target = head_cols((base + h) * group + g)
                    a_ref[:, target] = src[:, (2 * h * group + g) * HEAD : (2 * h * group + g + 1) * HEAD]
                    b_ref[:, target] = src[:, ((2 * h + 1) * group + g) * HEAD : ((2 * h + 1) * group + g + 1) * HEAD]
        first += heads


def unpack(info, pieces, chunks, members, group, heads_dev):
    rows = pieces[0].shape[0]
    width = members * heads_dev * group * HEAD
    return pl.pallas_call(
        functools.partial(unpack_kernel, chunks, members, group, heads_dev),
        out_shape=[jax.ShapeDtypeStruct((rows, width), BF16)] * 2,
        in_specs=[smem()] + [vmem()] * len(pieces),
        out_specs=[vmem()] * 2,
        compiler_params=pltpu.CompilerParams(vmem_limit_bytes=40 * 2**20),
        name="unpack",
    )(info, *pieces)


def attention_kernel(members, hops, group, rows, info, *refs):
    planes = hops + 1
    kv_refs = refs[:planes]
    q_refs = refs[planes : planes + members]
    o_refs = refs[planes + members : planes + 2 * members]
    dkv_refs = refs[planes + 2 * members : 2 * planes + 2 * members]
    k_s, v_s, kt_s, vt_s, dk_s, dv_s, q_s, o_s, p_all, eg_all, ds_all = refs[2 * planes + 2 * members :]
    me = info[0]
    plane = info[1]
    blocks = WINDOW // rows + 1
    wide = group * rows
    for k in range(planes):
        for s in range(members):
            at = (k * members + s) * rows
            piece = kv_refs[k][me ^ s]
            k_s[at : at + rows, :] = piece[:, :HEAD]
            v_s[at : at + rows, :] = piece[:, HEAD:]
            kt_s[:, at : at + rows] = piece[:, :HEAD].T
            vt_s[:, at : at + rows] = piece[:, HEAD:].T
    for m in range(members):
        q_s[m] = q_refs[m][...]
    key_at = lax.broadcasted_iota(jnp.int32, (rows, wide), 0)
    query_at = lax.broadcasted_iota(jnp.int32, (rows, wide), 1) % rows
    behind = key_at > query_at
    seen = [(plane >= hops - k).astype(F32) for k in range(planes)]
    pairs = [(b, min(b + JOIN, blocks)) for b in range(0, blocks, JOIN)]
    state = {}

    def forward(s):
        p_s, eg_s = p_all.at[s % BUFFERS], eg_all.at[s % BUFFERS]
        q_all = q_s[me ^ s]
        q = jnp.concatenate([q_all[:, g * HEAD : (g + 1) * HEAD] for g in range(group)], axis=0)
        go = jnp.concatenate([q_all[:, (group + g) * HEAD : (group + g + 1) * HEAD] for g in range(group)], axis=0)
        totals = [jnp.zeros((8, wide), F32) for _ in range(planes)]
        for low, high in pairs:
            scores = dot(k_s[(s + low) * rows : (s + high) * rows, :], q, 1, 1)
            for b in range(low, high):
                score = scores[(b - low) * rows : (b - low + 1) * rows]
                t = jnp.tanh(score * TANH_SCALE)
                e = jnp.exp2(t * EXP2_SCALE)
                if b == 0:
                    e = jnp.where(behind, e, 0.0)
                if b == blocks - 1:
                    e = jnp.where(behind, 0.0, e)
                k = (s + b) // members
                totals[k] = totals[k] + jnp.sum(e.reshape(rows // 8, 8, wide), axis=0)
                p_s[b * rows : (b + 1) * rows, :] = e.astype(BF16)
                eg_s[b * rows : (b + 1) * rows, :] = e * (1.0 - t * t)
            yield
        total = sum(jnp.sum(totals[k], axis=0, keepdims=True) * seen[k] for k in range(planes))
        inverse = 1.0 / total
        got = (go.astype(F32).T * inverse).astype(BF16)
        ot = dot(vt_s[:, s * rows : (s + blocks) * rows], p_s[...], 1, 0)
        ot = (ot * inverse).astype(BF16)
        gdot = jnp.sum(ot.astype(F32) * got.astype(F32), axis=0, keepdims=True)
        o = ot.astype(F32).T.astype(BF16)
        for g in range(group):
            o_s[me ^ s, :, g * HEAD : (g + 1) * HEAD] = o[g * rows : (g + 1) * rows]
        state[s] = (q, got, gdot)
        yield

    def inner(s):
        eg_s, ds_s = eg_all.at[s % BUFFERS], ds_all.at[s % BUFFERS]
        q, got, gdot = state[s]
        for low, high in pairs:
            dps = dot(v_s[(s + low) * rows : (s + high) * rows, :], got, 1, 0)
            part = slice(low * rows, high * rows)
            ds_s[part, :] = ((dps - gdot) * eg_s[part, :]).astype(BF16)
            yield

    def outer(s):
        p_s, ds_s = p_all.at[s % BUFFERS], ds_all.at[s % BUFFERS]
        q, got, gdot = state.pop(s)
        old = slice(s * rows, (s + blocks - 1) * rows)
        new = slice((s + blocks - 1) * rows, (s + blocks) * rows)

        def add(into, value):
            if s:
                into[old, :] += value[: (blocks - 1) * rows]
                into[new, :] = value[(blocks - 1) * rows :]
            else:
                into[: blocks * rows, :] = value

        add(dv_s, dot(p_s[...], got, 1, 1))
        yield
        add(dk_s, dot(ds_s[...], q, 1, 0))
        yield
        dqt = dot(kt_s[:, s * rows : (s + blocks) * rows], ds_s[...], 1, 0)
        dq = (dqt * SCORE_SCALE).T.astype(BF16)
        for g in range(group):
            o_s[me ^ s, :, (group + g) * HEAD : (group + g + 1) * HEAD] = dq[g * rows : (g + 1) * rows]
        yield

    def together(*walks):
        walks = list(walks)
        while walks:
            for walk in list(walks):
                if next(walk, walk) is walk:
                    walks.remove(walk)

    together(forward(0))
    for s in range(members):
        together(inner(s))
        together(*([forward(s + 1)] if s + 1 < members else []), outer(s))
    for m in range(members):
        o_refs[m][...] = o_s[m]
    for k in range(planes):
        for s in range(members):
            at = (k * members + s) * rows
            dkv_refs[k][me ^ s, :, :HEAD] = (dk_s[at : at + rows, :] * SCORE_SCALE).astype(BF16)
            dkv_refs[k][me ^ s, :, HEAD:] = dv_s[at : at + rows, :].astype(BF16)


def attention(info, kvs, qs, group, first=0, heads=None):
    planes, members = len(kvs), len(qs)
    rows = qs[0].shape[0]
    heads = heads or kvs[0].shape[2] // (2 * HEAD)
    keys_all = planes * members * rows
    wide = group * rows
    span = WINDOW + rows

    def kv_spec(start):
        return pl.BlockSpec((members, rows, 2 * HEAD), lambda h: (0, 0, h + start))

    def q_spec(start):
        return pl.BlockSpec((rows, 2 * group * HEAD), lambda h: (0, h + start))

    return pl.pallas_call(
        functools.partial(attention_kernel, members, planes - 1, group, rows),
        grid=(heads,),
        out_shape=[jax.ShapeDtypeStruct((rows, heads * 2 * group * HEAD), BF16)] * members
        + [jax.ShapeDtypeStruct((members, rows, heads * 2 * HEAD), BF16)] * planes,
        in_specs=[smem()] + [kv_spec(first)] * planes + [q_spec(first)] * members,
        out_specs=[q_spec(0)] * members + [kv_spec(0)] * planes,
        scratch_shapes=[
            pltpu.VMEM((keys_all, HEAD), BF16),
            pltpu.VMEM((keys_all, HEAD), BF16),
            pltpu.VMEM((HEAD, keys_all), BF16),
            pltpu.VMEM((HEAD, keys_all), BF16),
            pltpu.VMEM((keys_all, HEAD), F32),
            pltpu.VMEM((keys_all, HEAD), F32),
            pltpu.VMEM((members, rows, 2 * group * HEAD), BF16),
            pltpu.VMEM((members, rows, 2 * group * HEAD), BF16),
            pltpu.VMEM((BUFFERS, span, wide), BF16),
            pltpu.VMEM((BUFFERS, span, wide), F32),
            pltpu.VMEM((BUFFERS, span, wide), BF16),
        ],
        compiler_params=pltpu.CompilerParams(vmem_limit_bytes=40 * 2**20),
        cost_estimate=pl.CostEstimate(
            flops=12 * heads * members * wide * span * HEAD,
            bytes_accessed=2 * heads * members * rows * 4 * HEAD * (planes + group),
            transcendentals=2 * heads * members * wide * span,
        ),
        name="attention",
    )(info, *kvs, *qs)


def after(value, *earlier):
    leaves = [leaf for leaf in jax.tree.leaves(earlier)]
    return lax.optimization_barrier((value, leaves))[0] if leaves else value


def on_device(queries, keys, values, output_gradient):
    rows = queries.shape[0]
    tp = lax.axis_size("tp")
    ctx = lax.axis_size("ctx")
    members = INNER * tp
    heads_dev = keys.shape[1] // HEAD // members
    group = queries.shape[1] // keys.shape[1]
    hops = max(1, WINDOW // (members * rows))
    device = lax.axis_index("ctx") * tp + lax.axis_index("tp")
    info = jnp.stack([device % members, device // members]).astype(jnp.int32)
    axes = ("ctx", "tp")

    def swap(pieces):
        pairs = [[(i, i ^ m) for i in range(ctx * tp)] for m in range(members)]
        return [pieces[0]] + [lax.ppermute(pieces[m], axes, pairs[m]) for m in range(1, members)]

    def hop(array, by):
        pairs = [(i, i + by * members) for i in range(ctx * tp) if 0 <= i + by * members < ctx * tp]
        return lax.ppermute(array, axes, pairs)

    kv_packed = pack(info, keys, values, CHUNKS, members, 1, heads_dev)
    done = {}
    q_packed = []

    def gated(value, step):
        earlier = [done[name] for name in GATES.get(step, ()) if name in done]
        return after(value, *earlier)

    def run(step):
        kind, c = step[:-1], int(step[-1])
        if kind == "kv":
            done[step] = swap(gated(kv_packed[c * members : (c + 1) * members], step))
        elif kind == "q":
            if not q_packed:
                q_packed.extend(
                    pack(info, gated(queries, "pack"), output_gradient, CHUNKS, members, group, heads_dev)
                )
            done[step] = swap(gated(q_packed[c * members : (c + 1) * members], step))
        elif kind.startswith("z"):
            k = int(kind[1:])
            if k == 1:
                done[f"z0{c}"] = jnp.stack(done[f"kv{c}"])
            done[step] = hop(gated(done[f"z{k - 1}{c}"], step), 1)
        elif kind == "att":
            part, first, heads = CALLS[c]
            halo = [done[f"z{k}{part}"] for k in range(hops, -1, -1)]
            halo, pieces = gated((halo, done[f"q{part}"]), step)
            results = attention(info, halo, pieces, group, first, heads)
            done[step] = results[members:]
            done[f"os{c}"] = results[:members]
            done[f"r0{c}"] = results[members]
        elif kind == "o":
            done[step] = swap(gated(done[f"os{c}"], step))
        elif kind.startswith("r"):
            k = int(kind[1:])
            arrived = hop(gated(done[f"r{k - 1}{c}"], step), -1)
            done[step] = (arrived.astype(F32) + done[f"att{c}"][k].astype(F32)).astype(BF16)
        else:
            carried = gated(done[f"r{hops}{c}"], step)
            done[step] = swap([carried[m] for m in range(members)])

    for step in STEPS:
        kind = step[:-1]
        if kind in ("z", "r"):
            for k in range(1, hops + 1):
                run(f"{kind}{k}{step[-1]}")
        else:
            run(step)
    returned = [heads for _, _, heads in CALLS]
    o_all = sum([done[f"o{c}"] for c in range(len(CALLS))], [])
    dkv_all = sum([done[f"dx{c}"] for c in range(len(CALLS))], [])
    attended, query_grad = unpack(info, o_all, returned, members, group, heads_dev)
    key_grad, value_grad = unpack(info, dkv_all, returned, members, 1, heads_dev)
    return attended, query_grad, key_grad, value_grad


def solution(mesh):
    placed = P(("group", "ctx", "tp"), None)
    return jax.shard_map(
        on_device, mesh=mesh, in_specs=(placed,) * 4, out_specs=(placed,) * 4, check_vma=False
    )
```

```python
import functools
import math

import jax
import jax.numpy as jnp
from jax import lax
from jax.experimental import pallas as pl
from jax.experimental.pallas import tpu as pltpu
from jax.sharding import PartitionSpec as P

HEAD = 128
WINDOW = 1024
INNER = 2
CHUNKS = (2, 2)
CALLS = ((0, 0, 2), (1, 0, 2))
DIRECT_IN = ()
DIRECT_OUT = (1,)
STEPS = ("kv0", "kv1", "z0", "q0", "q1", "z1", "att0", "o0", "r0", "dx0", "att1", "o1", "dx1", "r1")
GATES = {
    "kv1": ("kv0",),
    "pack": ("kv0",),
    "q1": ("q0",),
    "r11": ("o0",),
    "r21": ("o1", "dx1"),
}
SOFTCAP = 50.0
TANH_SCALE = 1.0 / (12.0 * SOFTCAP)
EXP2_SCALE = SOFTCAP * math.log2(math.e)
SCORE_SCALE = 1.0 / 12.0
F32 = jnp.float32
BF16 = jnp.bfloat16
BUFFERS = 2
JOIN = 3


def dot(a, b, ca, cb):
    return lax.dot_general(a, b, (((ca,), (cb,)), ((), ())), preferred_element_type=F32)


def vmem():
    return pl.BlockSpec(memory_space=pltpu.VMEM)


def smem():
    return pl.BlockSpec(memory_space=pltpu.SMEM)


def head_cols(index):
    return pl.ds(pl.multiple_of(index * HEAD, HEAD), HEAD)


def pack_kernel(chunks, members, group, heads_dev, info, a_ref, b_ref, *outs):
    me = info[0]
    first = 0
    for c, heads in enumerate(chunks):
        for m in range(members):
            out = outs[c * members + m]
            base = (me ^ m) * heads_dev + first
            for h in range(heads):
                for g in range(group):
                    source = head_cols((base + h) * group + g)
                    out[:, (2 * h * group + g) * HEAD : (2 * h * group + g + 1) * HEAD] = a_ref[:, source]
                    out[:, ((2 * h + 1) * group + g) * HEAD : ((2 * h + 1) * group + g + 1) * HEAD] = b_ref[:, source]
        first += heads


def pack(info, a, b, chunks, members, group, heads_dev):
    rows = a.shape[0]
    return pl.pallas_call(
        functools.partial(pack_kernel, chunks, members, group, heads_dev),
        out_shape=[
            jax.ShapeDtypeStruct((rows, 2 * h * group * HEAD), BF16) for h in chunks for _ in range(members)
        ],
        in_specs=[smem(), vmem(), vmem()],
        out_specs=[vmem()] * (len(chunks) * members),
        compiler_params=pltpu.CompilerParams(vmem_limit_bytes=40 * 2**20),
        name="pack",
    )(info, a, b)


def unpack_kernel(chunks, members, group, heads_dev, later, info, *refs):
    me = info[0]
    count = len(chunks) * members
    ins, more, (a_ref, b_ref) = refs[:count], dict(zip(later, refs[count:-2])), refs[-2:]
    first = 0
    for c, heads in enumerate(chunks):
        for m in range(members):
            at = c * members + m
            base = (me ^ m) * heads_dev + first

            def block(column):
                part = slice(column * HEAD, (column + 1) * HEAD)
                if at not in more:
                    return ins[at][:, part]
                return (ins[at][:, part].astype(F32) + more[at][:, part].astype(F32)).astype(BF16)

            for h in range(heads):
                for g in range(group):
                    target = head_cols((base + h) * group + g)
                    a_ref[:, target] = block(2 * h * group + g)
                    b_ref[:, target] = block((2 * h + 1) * group + g)
        first += heads


def unpack(info, pieces, later, chunks, members, group, heads_dev):
    rows = pieces[0].shape[0]
    width = members * heads_dev * group * HEAD
    where = tuple(later)
    more = [later[at] for at in where]
    return pl.pallas_call(
        functools.partial(unpack_kernel, chunks, members, group, heads_dev, where),
        out_shape=[jax.ShapeDtypeStruct((rows, width), BF16)] * 2,
        in_specs=[smem()] + [vmem()] * (len(pieces) + len(more)),
        out_specs=[vmem()] * 2,
        compiler_params=pltpu.CompilerParams(vmem_limit_bytes=40 * 2**20),
        name="unpack",
    )(info, *pieces, *more)


def attention_kernel(members, hops, group, rows, info, *refs):
    planes = hops + 1
    kv_refs = refs[:planes]
    q_refs = refs[planes : planes + members]
    o_refs = refs[planes + members : planes + 2 * members]
    dkv_refs = refs[planes + 2 * members : 2 * planes + 2 * members]
    k_s, v_s, kt_s, vt_s, dk_s, dv_s, q_s, o_s, p_all, eg_all, ds_all = refs[2 * planes + 2 * members :]
    me = info[0]
    plane = info[1]
    blocks = WINDOW // rows + 1
    wide = group * rows
    for k in range(planes):
        for s in range(members):
            at = (k * members + s) * rows
            piece = kv_refs[k][me ^ s]
            k_s[at : at + rows, :] = piece[:, :HEAD]
            v_s[at : at + rows, :] = piece[:, HEAD:]
            kt_s[:, at : at + rows] = piece[:, :HEAD].T
            vt_s[:, at : at + rows] = piece[:, HEAD:].T
    for m in range(members):
        q_s[m] = q_refs[m][...]
    key_at = lax.broadcasted_iota(jnp.int32, (rows, wide), 0)
    query_at = lax.broadcasted_iota(jnp.int32, (rows, wide), 1) % rows
    behind = key_at > query_at
    seen = [(plane >= hops - k).astype(F32) for k in range(planes)]
    pairs = [(b, min(b + JOIN, blocks)) for b in range(0, blocks, JOIN)]
    state = {}

    def forward(s):
        p_s, eg_s = p_all.at[s % BUFFERS], eg_all.at[s % BUFFERS]
        q_all = q_s[me ^ s]
        q = jnp.concatenate([q_all[:, g * HEAD : (g + 1) * HEAD] for g in range(group)], axis=0)
        go = jnp.concatenate([q_all[:, (group + g) * HEAD : (group + g + 1) * HEAD] for g in range(group)], axis=0)
        totals = [jnp.zeros((8, wide), F32) for _ in range(planes)]
        for low, high in pairs:
            scores = dot(k_s[(s + low) * rows : (s + high) * rows, :], q, 1, 1)
            for b in range(low, high):
                score = scores[(b - low) * rows : (b - low + 1) * rows]
                t = jnp.tanh(score * TANH_SCALE)
                e = jnp.exp2(t * EXP2_SCALE)
                if b == 0:
                    e = jnp.where(behind, e, 0.0)
                if b == blocks - 1:
                    e = jnp.where(behind, 0.0, e)
                k = (s + b) // members
                totals[k] = totals[k] + jnp.sum(e.reshape(rows // 8, 8, wide), axis=0)
                p_s[b * rows : (b + 1) * rows, :] = e.astype(BF16)
                eg_s[b * rows : (b + 1) * rows, :] = e * (1.0 - t * t)
            yield
        total = sum(jnp.sum(totals[k], axis=0, keepdims=True) * seen[k] for k in range(planes))
        inverse = 1.0 / total
        got = (go.astype(F32).T * inverse).astype(BF16)
        ot = dot(vt_s[:, s * rows : (s + blocks) * rows], p_s[...], 1, 0)
        ot = (ot * inverse).astype(BF16)
        gdot = jnp.sum(ot.astype(F32) * got.astype(F32), axis=0, keepdims=True)
        o = ot.astype(F32).T.astype(BF16)
        for g in range(group):
            o_s[me ^ s, :, g * HEAD : (g + 1) * HEAD] = o[g * rows : (g + 1) * rows]
        state[s] = (q, got, gdot)
        yield

    def inner(s):
        eg_s, ds_s = eg_all.at[s % BUFFERS], ds_all.at[s % BUFFERS]
        q, got, gdot = state[s]
        for low, high in pairs:
            dps = dot(v_s[(s + low) * rows : (s + high) * rows, :], got, 1, 0)
            part = slice(low * rows, high * rows)
            ds_s[part, :] = ((dps - gdot) * eg_s[part, :]).astype(BF16)
            yield

    def outer(s):
        p_s, ds_s = p_all.at[s % BUFFERS], ds_all.at[s % BUFFERS]
        q, got, gdot = state.pop(s)
        old = slice(s * rows, (s + blocks - 1) * rows)
        new = slice((s + blocks - 1) * rows, (s + blocks) * rows)

        def add(into, value):
            if s:
                into[old, :] += value[: (blocks - 1) * rows]
                into[new, :] = value[(blocks - 1) * rows :]
            else:
                into[: blocks * rows, :] = value

        add(dv_s, dot(p_s[...], got, 1, 1))
        yield
        add(dk_s, dot(ds_s[...], q, 1, 0))
        yield
        dqt = dot(kt_s[:, s * rows : (s + blocks) * rows], ds_s[...], 1, 0)
        dq = (dqt * SCORE_SCALE).T.astype(BF16)
        for g in range(group):
            o_s[me ^ s, :, (group + g) * HEAD : (group + g + 1) * HEAD] = dq[g * rows : (g + 1) * rows]
        yield

    def together(*walks):
        walks = list(walks)
        while walks:
            for walk in list(walks):
                if next(walk, walk) is walk:
                    walks.remove(walk)

    together(forward(0))
    for s in range(members):
        together(inner(s))
        together(*([forward(s + 1)] if s + 1 < members else []), outer(s))
    for m in range(members):
        o_refs[m][...] = o_s[m]
    for k in range(planes):
        for s in range(members):
            at = (k * members + s) * rows
            dkv_refs[k][me ^ s, :, :HEAD] = (dk_s[at : at + rows, :] * SCORE_SCALE).astype(BF16)
            dkv_refs[k][me ^ s, :, HEAD:] = dv_s[at : at + rows, :].astype(BF16)


def attention(info, kvs, qs, group, first=0, heads=None):
    planes, members = len(kvs), len(qs)
    rows = qs[0].shape[0]
    heads = heads or kvs[0].shape[2] // (2 * HEAD)
    keys_all = planes * members * rows
    wide = group * rows
    span = WINDOW + rows

    def kv_spec(start):
        return pl.BlockSpec((members, rows, 2 * HEAD), lambda h: (0, 0, h + start))

    def q_spec(start):
        return pl.BlockSpec((rows, 2 * group * HEAD), lambda h: (0, h + start))

    return pl.pallas_call(
        functools.partial(attention_kernel, members, planes - 1, group, rows),
        grid=(heads,),
        out_shape=[jax.ShapeDtypeStruct((rows, heads * 2 * group * HEAD), BF16)] * members
        + [jax.ShapeDtypeStruct((members, rows, heads * 2 * HEAD), BF16)] * planes,
        in_specs=[smem()] + [kv_spec(first)] * planes + [q_spec(first)] * members,
        out_specs=[q_spec(0)] * members + [kv_spec(0)] * planes,
        scratch_shapes=[
            pltpu.VMEM((keys_all, HEAD), BF16),
            pltpu.VMEM((keys_all, HEAD), BF16),
            pltpu.VMEM((HEAD, keys_all), BF16),
            pltpu.VMEM((HEAD, keys_all), BF16),
            pltpu.VMEM((keys_all, HEAD), F32),
            pltpu.VMEM((keys_all, HEAD), F32),
            pltpu.VMEM((members, rows, 2 * group * HEAD), BF16),
            pltpu.VMEM((members, rows, 2 * group * HEAD), BF16),
            pltpu.VMEM((BUFFERS, span, wide), BF16),
            pltpu.VMEM((BUFFERS, span, wide), F32),
            pltpu.VMEM((BUFFERS, span, wide), BF16),
        ],
        compiler_params=pltpu.CompilerParams(vmem_limit_bytes=40 * 2**20),
        cost_estimate=pl.CostEstimate(
            flops=12 * heads * members * wide * span * HEAD,
            bytes_accessed=2 * heads * members * rows * 4 * HEAD * (planes + group),
            transcendentals=2 * heads * members * wide * span,
        ),
        name="attention",
    )(info, *kvs, *qs)


def after(value, *earlier):
    leaves = [leaf for leaf in jax.tree.leaves(earlier)]
    return lax.optimization_barrier((value, leaves))[0] if leaves else value


def on_device(queries, keys, values, output_gradient):
    rows = queries.shape[0]
    tp = lax.axis_size("tp")
    ctx = lax.axis_size("ctx")
    members = INNER * tp
    heads_dev = keys.shape[1] // HEAD // members
    group = queries.shape[1] // keys.shape[1]
    hops = max(1, WINDOW // (members * rows))
    device = lax.axis_index("ctx") * tp + lax.axis_index("tp")
    info = jnp.stack([device % members, device // members]).astype(jnp.int32)
    axes = ("ctx", "tp")

    def swap(pieces):
        pairs = [[(i, i ^ m) for i in range(ctx * tp)] for m in range(members)]
        return [pieces[0]] + [lax.ppermute(pieces[m], axes, pairs[m]) for m in range(1, members)]

    def hop(array, by):
        pairs = [(i, i + by * members) for i in range(ctx * tp) if 0 <= i + by * members < ctx * tp]
        return lax.ppermute(array, axes, pairs)

    def hop_across(pieces, by):
        count = ctx * tp
        pairs = [
            [(i, (i ^ m) + by * members) for i in range(count) if 0 <= (i ^ m) + by * members < count]
            for m in range(members)
        ]
        return [lax.ppermute(pieces[m], axes, pairs[m]) for m in range(members)]

    kv_packed = pack(info, keys, values, CHUNKS, members, 1, heads_dev)
    done = {}
    q_packed = []

    def gated(value, step):
        earlier = [done[name] for name in GATES.get(step, ()) if name in done]
        return after(value, *earlier)

    def run(step):
        kind, c = step[:-1], int(step[-1])
        if kind == "kv":
            done[step] = swap(gated(kv_packed[c * members : (c + 1) * members], step))
        elif kind == "q":
            if not q_packed:
                q_packed.extend(
                    pack(info, gated(queries, "pack"), output_gradient, CHUNKS, members, group, heads_dev)
                )
            done[step] = swap(gated(q_packed[c * members : (c + 1) * members], step))
        elif kind.startswith("z"):
            k = int(kind[1:])
            if k == 1 and c in DIRECT_IN:
                pieces = hop_across(gated(kv_packed[c * members : (c + 1) * members], step), 1)
                done[f"first{c}"] = pieces[0]
                done[step] = jnp.stack(pieces)
            else:
                if k == 1:
                    done[f"z0{c}"] = jnp.stack(done[f"kv{c}"])
                done[step] = hop(gated(done[f"z{k - 1}{c}"], step), 1)
        elif kind == "att":
            part, first, heads = CALLS[c]
            if f"z0{part}" not in done:
                done[f"z0{part}"] = jnp.stack(done[f"kv{part}"])
            halo = [done[f"z{k}{part}"] for k in range(hops, -1, -1)]
            halo, pieces = gated((halo, done[f"q{part}"]), step)
            results = attention(info, halo, pieces, group, first, heads)
            done[step] = results[members:]
            done[f"os{c}"] = results[:members]
            done[f"r0{c}"] = results[members]
        elif kind == "o":
            done[step] = swap(gated(done[f"os{c}"], step))
        elif kind.startswith("r"):
            k = int(kind[1:])
            carried = gated(done[f"r{k - 1}{c}"], step)
            if k == hops and c in DIRECT_OUT:
                done[step] = hop_across([carried[m] for m in range(members)], -1)
                return
            arrived = hop(carried, -1)
            done[step] = (arrived.astype(F32) + done[f"att{c}"][k].astype(F32)).astype(BF16)
        else:
            carried = gated(done[f"att{c}"][hops] if c in DIRECT_OUT else done[f"r{hops}{c}"], step)
            done[step] = swap([carried[m] for m in range(members)])

    for step in STEPS:
        kind = step[:-1]
        if kind in ("z", "r"):
            for k in range(1, hops + 1):
                run(f"{kind}{k}{step[-1]}")
        else:
            run(step)
    returned = [heads for _, _, heads in CALLS]
    o_all = sum([done[f"o{c}"] for c in range(len(CALLS))], [])
    dkv_all = sum([done[f"dx{c}"] for c in range(len(CALLS))], [])
    attended, query_grad = unpack(info, o_all, {}, returned, members, group, heads_dev)
    later = {c * members + m: done[f"r{hops}{c}"][m] for c in DIRECT_OUT for m in range(members)}
    key_grad, value_grad = unpack(info, dkv_all, later, returned, members, 1, heads_dev)
    return attended, query_grad, key_grad, value_grad


def solution(mesh):
    placed = P(("group", "ctx", "tp"), None)
    return jax.shard_map(
        on_device, mesh=mesh, in_specs=(placed,) * 4, out_specs=(placed,) * 4, check_vma=False
    )
```

```python
import functools
import math

import jax
import jax.numpy as jnp
from jax import lax
from jax.experimental import pallas as pl
from jax.experimental.pallas import tpu as pltpu
from jax.sharding import PartitionSpec as P

HEAD = 128
WINDOW = 1024
INNER = 2
CHUNKS = (2, 2)
CALLS = ((0, 0, 2), (1, 0, 2))
DIRECT_IN = ()
DIRECT_OUT = (1,)
STEPS = ("kv0", "kv1", "z0", "q0", "q1", "z1", "att0", "o0", "r0", "dx0", "att1", "o1", "dx1", "r1")
GATES = {
    "kv1": ("kv0",),
    "pack": ("kv0",),
    "q1": ("q0",),
    "r11": ("o0",),
    "r21": ("o1", "dx1"),
}
SOFTCAP = 50.0
TANH_SCALE = 1.0 / (12.0 * SOFTCAP)
EXP2_SCALE = SOFTCAP * math.log2(math.e)
SCORE_SCALE = 1.0 / 12.0
F32 = jnp.float32
BF16 = jnp.bfloat16
BUFFERS = 2
JOIN = 3


def dot(a, b, ca, cb):
    return lax.dot_general(a, b, (((ca,), (cb,)), ((), ())), preferred_element_type=F32)


def vmem():
    return pl.BlockSpec(memory_space=pltpu.VMEM)


def smem():
    return pl.BlockSpec(memory_space=pltpu.SMEM)


def head_cols(index):
    return pl.ds(pl.multiple_of(index * HEAD, HEAD), HEAD)


def pack_kernel(chunks, members, group, heads_dev, info, a_ref, b_ref, *outs):
    me = info[0]
    first = 0
    for c, heads in enumerate(chunks):
        for m in range(members):
            out = outs[c * members + m]
            base = (me ^ m) * heads_dev + first
            for h in range(heads):
                for g in range(group):
                    source = head_cols((base + h) * group + g)
                    out[:, (2 * h * group + g) * HEAD : (2 * h * group + g + 1) * HEAD] = a_ref[:, source]
                    out[:, ((2 * h + 1) * group + g) * HEAD : ((2 * h + 1) * group + g + 1) * HEAD] = b_ref[:, source]
        first += heads


def pack(info, a, b, chunks, members, group, heads_dev):
    rows = a.shape[0]
    return pl.pallas_call(
        functools.partial(pack_kernel, chunks, members, group, heads_dev),
        out_shape=[
            jax.ShapeDtypeStruct((rows, 2 * h * group * HEAD), BF16) for h in chunks for _ in range(members)
        ],
        in_specs=[smem(), vmem(), vmem()],
        out_specs=[vmem()] * (len(chunks) * members),
        compiler_params=pltpu.CompilerParams(vmem_limit_bytes=40 * 2**20),
        name="pack",
    )(info, a, b)


def unpack_kernel(chunks, members, group, heads_dev, later, info, *refs):
    me = info[0]
    count = len(chunks) * members
    ins, more, (a_ref, b_ref) = refs[:count], dict(zip(later, refs[count:-2])), refs[-2:]
    first = 0
    for c, heads in enumerate(chunks):
        for m in range(members):
            at = c * members + m
            base = (me ^ m) * heads_dev + first

            def block(column):
                part = slice(column * HEAD, (column + 1) * HEAD)
                if at not in more:
                    return ins[at][:, part]
                return (ins[at][:, part].astype(F32) + more[at][:, part].astype(F32)).astype(BF16)

            for h in range(heads):
                for g in range(group):
                    target = head_cols((base + h) * group + g)
                    a_ref[:, target] = block(2 * h * group + g)
                    b_ref[:, target] = block((2 * h + 1) * group + g)
        first += heads


def unpack(info, pieces, later, chunks, members, group, heads_dev):
    rows = pieces[0].shape[0]
    width = members * heads_dev * group * HEAD
    where = tuple(later)
    more = [later[at] for at in where]
    return pl.pallas_call(
        functools.partial(unpack_kernel, chunks, members, group, heads_dev, where),
        out_shape=[jax.ShapeDtypeStruct((rows, width), BF16)] * 2,
        in_specs=[smem()] + [vmem()] * (len(pieces) + len(more)),
        out_specs=[vmem()] * 2,
        compiler_params=pltpu.CompilerParams(vmem_limit_bytes=40 * 2**20),
        name="unpack",
    )(info, *pieces, *more)


def attention_kernel(members, hops, group, rows, heads, info, *refs):
    planes = hops + 1
    kv_refs = refs[:planes]
    q_refs = refs[planes : planes + members]
    o_refs = refs[planes + members : planes + 2 * members]
    dkv_refs = refs[planes + 2 * members : 2 * planes + 2 * members]
    k_all, v_all, kt_all, vt_all, dk_all, dv_all, q_s, o_s, p_all, eg_all, ds_all = refs[2 * planes + 2 * members :]
    me = info[0]
    plane = info[1]
    blocks = WINDOW // rows + 1
    wide = group * rows
    wide_q = 2 * group * HEAD
    key_at = lax.broadcasted_iota(jnp.int32, (rows, wide), 0)
    query_at = lax.broadcasted_iota(jnp.int32, (rows, wide), 1) % rows
    behind = key_at > query_at
    seen = [(plane >= hops - k).astype(F32) for k in range(planes)]
    pairs = [(b, min(b + JOIN, blocks)) for b in range(0, blocks, JOIN)]
    state = {}

    def prepare(h):
        k_s, v_s, kt_s, vt_s = k_all.at[h % BUFFERS], v_all.at[h % BUFFERS], kt_all.at[h % BUFFERS], vt_all.at[h % BUFFERS]
        for m in range(members):
            q_s[h, m] = q_refs[m][:, h * wide_q : (h + 1) * wide_q]
        for k in range(planes):
            for s in range(members):
                at = (k * members + s) * rows
                keys = kv_refs[k][me ^ s, :, 2 * h * HEAD : (2 * h + 1) * HEAD]
                values = kv_refs[k][me ^ s, :, (2 * h + 1) * HEAD : (2 * h + 2) * HEAD]
                k_s[at : at + rows, :] = keys
                v_s[at : at + rows, :] = values
                kt_s[:, at : at + rows] = keys.T
                vt_s[:, at : at + rows] = values.T
            yield

    def forward(h, s):
        turn = (h * members + s) % BUFFERS
        k_s, vt_s = k_all.at[h % BUFFERS], vt_all.at[h % BUFFERS]
        p_s, eg_s = p_all.at[turn], eg_all.at[turn]
        q_all = q_s[h, me ^ s]
        q = jnp.concatenate([q_all[:, g * HEAD : (g + 1) * HEAD] for g in range(group)], axis=0)
        go = jnp.concatenate([q_all[:, (group + g) * HEAD : (group + g + 1) * HEAD] for g in range(group)], axis=0)
        totals = [jnp.zeros((8, wide), F32) for _ in range(planes)]
        for low, high in pairs:
            scores = dot(k_s[(s + low) * rows : (s + high) * rows, :], q, 1, 1)
            for b in range(low, high):
                score = scores[(b - low) * rows : (b - low + 1) * rows]
                t = jnp.tanh(score * TANH_SCALE)
                e = jnp.exp2(t * EXP2_SCALE)
                if b == 0:
                    e = jnp.where(behind, e, 0.0)
                if b == blocks - 1:
                    e = jnp.where(behind, 0.0, e)
                k = (s + b) // members
                totals[k] = totals[k] + jnp.sum(e.reshape(rows // 8, 8, wide), axis=0)
                p_s[b * rows : (b + 1) * rows, :] = e.astype(BF16)
                eg_s[b * rows : (b + 1) * rows, :] = e * (1.0 - t * t)
            yield
        total = sum(jnp.sum(totals[k], axis=0, keepdims=True) * seen[k] for k in range(planes))
        inverse = 1.0 / total
        got = (go.astype(F32).T * inverse).astype(BF16)
        ot = dot(vt_s[:, s * rows : (s + blocks) * rows], p_s[...], 1, 0)
        ot = (ot * inverse).astype(BF16)
        gdot = jnp.sum(ot.astype(F32) * got.astype(F32), axis=0, keepdims=True)
        o = ot.astype(F32).T.astype(BF16)
        for g in range(group):
            o_s[h, me ^ s, :, g * HEAD : (g + 1) * HEAD] = o[g * rows : (g + 1) * rows]
        state[h, s] = (q, got, gdot)
        yield

    def inner(h, s):
        turn = (h * members + s) % BUFFERS
        v_s, eg_s, ds_s = v_all.at[h % BUFFERS], eg_all.at[turn], ds_all.at[turn]
        q, got, gdot = state[h, s]
        for low, high in pairs:
            dps = dot(v_s[(s + low) * rows : (s + high) * rows, :], got, 1, 0)
            part = slice(low * rows, high * rows)
            ds_s[part, :] = ((dps - gdot) * eg_s[part, :]).astype(BF16)
            yield

    def outer(h, s):
        turn = (h * members + s) % BUFFERS
        kt_s, dk_s, dv_s = kt_all.at[h % BUFFERS], dk_all.at[h % BUFFERS], dv_all.at[h % BUFFERS]
        p_s, ds_s = p_all.at[turn], ds_all.at[turn]
        q, got, gdot = state.pop((h, s))
        old = slice(s * rows, (s + blocks - 1) * rows)
        new = slice((s + blocks - 1) * rows, (s + blocks) * rows)

        def add(into, value):
            if s:
                into[old, :] += value[: (blocks - 1) * rows]
                into[new, :] = value[(blocks - 1) * rows :]
            else:
                into[: blocks * rows, :] = value

        add(dv_s, dot(p_s[...], got, 1, 1))
        yield
        add(dk_s, dot(ds_s[...], q, 1, 0))
        yield
        dqt = dot(kt_s[:, s * rows : (s + blocks) * rows], ds_s[...], 1, 0)
        dq = (dqt * SCORE_SCALE).T.astype(BF16)
        for g in range(group):
            o_s[h, me ^ s, :, (group + g) * HEAD : (group + g + 1) * HEAD] = dq[g * rows : (g + 1) * rows]
        yield

    def finish(h):
        dk_s, dv_s = dk_all.at[h % BUFFERS], dv_all.at[h % BUFFERS]
        for k in range(planes):
            for s in range(members):
                at = (k * members + s) * rows
                keys = (dk_s[at : at + rows, :] * SCORE_SCALE).astype(BF16)
                dkv_refs[k][me ^ s, :, 2 * h * HEAD : (2 * h + 1) * HEAD] = keys
                dkv_refs[k][me ^ s, :, (2 * h + 1) * HEAD : (2 * h + 2) * HEAD] = dv_s[at : at + rows, :].astype(BF16)
            yield
        for m in range(members):
            o_refs[m][:, h * wide_q : (h + 1) * wide_q] = o_s[h, m]

    def together(*walks):
        walks = list(walks)
        while walks:
            for walk in list(walks):
                if next(walk, walk) is walk:
                    walks.remove(walk)

    tiles = [(h, s) for h in range(heads) for s in range(members)]
    together(prepare(0))
    together(forward(0, 0))
    for i, (h, s) in enumerate(tiles):
        together(inner(h, s))
        beside = [outer(h, s)]
        if i + 1 < len(tiles):
            beside.insert(0, forward(*tiles[i + 1]))
        if s == 1 and h + 1 < heads:
            beside.append(prepare(h + 1))
        if s == 0 and h > 0:
            beside.append(finish(h - 1))
        together(*beside)
    together(finish(heads - 1))


def attention(info, kvs, qs, group, first=0, heads=None):
    planes, members = len(kvs), len(qs)
    rows = qs[0].shape[0]
    heads = kvs[0].shape[2] // (2 * HEAD)
    keys_all = planes * members * rows
    wide = group * rows
    span = WINDOW + rows
    return pl.pallas_call(
        functools.partial(attention_kernel, members, planes - 1, group, rows, heads),
        out_shape=[jax.ShapeDtypeStruct(q.shape, BF16) for q in qs]
        + [jax.ShapeDtypeStruct(kv.shape, BF16) for kv in kvs],
        in_specs=[smem()] + [vmem()] * (planes + members),
        out_specs=[vmem()] * (planes + members),
        scratch_shapes=[
            pltpu.VMEM((BUFFERS, keys_all, HEAD), BF16),
            pltpu.VMEM((BUFFERS, keys_all, HEAD), BF16),
            pltpu.VMEM((BUFFERS, HEAD, keys_all), BF16),
            pltpu.VMEM((BUFFERS, HEAD, keys_all), BF16),
            pltpu.VMEM((BUFFERS, keys_all, HEAD), F32),
            pltpu.VMEM((BUFFERS, keys_all, HEAD), F32),
            pltpu.VMEM((heads, members, rows, 2 * group * HEAD), BF16),
            pltpu.VMEM((heads, members, rows, 2 * group * HEAD), BF16),
            pltpu.VMEM((BUFFERS, span, wide), BF16),
            pltpu.VMEM((BUFFERS, span, wide), F32),
            pltpu.VMEM((BUFFERS, span, wide), BF16),
        ],
        compiler_params=pltpu.CompilerParams(vmem_limit_bytes=40 * 2**20),
        cost_estimate=pl.CostEstimate(
            flops=12 * heads * members * wide * span * HEAD,
            bytes_accessed=2 * heads * members * rows * 4 * HEAD * (planes + group),
            transcendentals=2 * heads * members * wide * span,
        ),
        name="attention",
    )(info, *kvs, *qs)


def after(value, *earlier):
    leaves = [leaf for leaf in jax.tree.leaves(earlier)]
    return lax.optimization_barrier((value, leaves))[0] if leaves else value


def on_device(queries, keys, values, output_gradient):
    rows = queries.shape[0]
    tp = lax.axis_size("tp")
    ctx = lax.axis_size("ctx")
    members = INNER * tp
    heads_dev = keys.shape[1] // HEAD // members
    group = queries.shape[1] // keys.shape[1]
    hops = max(1, WINDOW // (members * rows))
    device = lax.axis_index("ctx") * tp + lax.axis_index("tp")
    info = jnp.stack([device % members, device // members]).astype(jnp.int32)
    axes = ("ctx", "tp")

    def swap(pieces):
        pairs = [[(i, i ^ m) for i in range(ctx * tp)] for m in range(members)]
        return [pieces[0]] + [lax.ppermute(pieces[m], axes, pairs[m]) for m in range(1, members)]

    def hop(array, by):
        pairs = [(i, i + by * members) for i in range(ctx * tp) if 0 <= i + by * members < ctx * tp]
        return lax.ppermute(array, axes, pairs)

    def hop_across(pieces, by):
        count = ctx * tp
        pairs = [
            [(i, (i ^ m) + by * members) for i in range(count) if 0 <= (i ^ m) + by * members < count]
            for m in range(members)
        ]
        return [lax.ppermute(pieces[m], axes, pairs[m]) for m in range(members)]

    kv_packed = pack(info, keys, values, CHUNKS, members, 1, heads_dev)
    done = {}
    q_packed = []

    def gated(value, step):
        earlier = [done[name] for name in GATES.get(step, ()) if name in done]
        return after(value, *earlier)

    def run(step):
        kind, c = step[:-1], int(step[-1])
        if kind == "kv":
            done[step] = swap(gated(kv_packed[c * members : (c + 1) * members], step))
        elif kind == "q":
            if not q_packed:
                q_packed.extend(
                    pack(info, gated(queries, "pack"), output_gradient, CHUNKS, members, group, heads_dev)
                )
            done[step] = swap(gated(q_packed[c * members : (c + 1) * members], step))
        elif kind.startswith("z"):
            k = int(kind[1:])
            if k == 1 and c in DIRECT_IN:
                pieces = hop_across(gated(kv_packed[c * members : (c + 1) * members], step), 1)
                done[f"first{c}"] = pieces[0]
                done[step] = jnp.stack(pieces)
            else:
                if k == 1:
                    done[f"z0{c}"] = jnp.stack(done[f"kv{c}"])
                done[step] = hop(gated(done[f"z{k - 1}{c}"], step), 1)
        elif kind == "att":
            part, first, heads = CALLS[c]
            if f"z0{part}" not in done:
                done[f"z0{part}"] = jnp.stack(done[f"kv{part}"])
            halo = [done[f"z{k}{part}"] for k in range(hops, -1, -1)]
            halo, pieces = gated((halo, done[f"q{part}"]), step)
            results = attention(info, halo, pieces, group, first, heads)
            done[step] = results[members:]
            done[f"os{c}"] = results[:members]
            done[f"r0{c}"] = results[members]
        elif kind == "o":
            done[step] = swap(gated(done[f"os{c}"], step))
        elif kind.startswith("r"):
            k = int(kind[1:])
            carried = gated(done[f"r{k - 1}{c}"], step)
            if k == hops and c in DIRECT_OUT:
                done[step] = hop_across([carried[m] for m in range(members)], -1)
                return
            arrived = hop(carried, -1)
            done[step] = (arrived.astype(F32) + done[f"att{c}"][k].astype(F32)).astype(BF16)
        else:
            carried = gated(done[f"att{c}"][hops] if c in DIRECT_OUT else done[f"r{hops}{c}"], step)
            done[step] = swap([carried[m] for m in range(members)])

    for step in STEPS:
        kind = step[:-1]
        if kind in ("z", "r"):
            for k in range(1, hops + 1):
                run(f"{kind}{k}{step[-1]}")
        else:
            run(step)
    returned = [heads for _, _, heads in CALLS]
    o_all = sum([done[f"o{c}"] for c in range(len(CALLS))], [])
    dkv_all = sum([done[f"dx{c}"] for c in range(len(CALLS))], [])
    attended, query_grad = unpack(info, o_all, {}, returned, members, group, heads_dev)
    later = {c * members + m: done[f"r{hops}{c}"][m] for c in DIRECT_OUT for m in range(members)}
    key_grad, value_grad = unpack(info, dkv_all, later, returned, members, 1, heads_dev)
    return attended, query_grad, key_grad, value_grad


def solution(mesh):
    placed = P(("group", "ctx", "tp"), None)
    return jax.shard_map(
        on_device, mesh=mesh, in_specs=(placed,) * 4, out_specs=(placed,) * 4, check_vma=False
    )
```

```python
import functools
import math

import jax
import jax.numpy as jnp
from jax import lax
from jax.experimental import pallas as pl
from jax.experimental.pallas import tpu as pltpu
from jax.sharding import PartitionSpec as P

HEAD = 128
WINDOW = 1024
INNER = 2
CHUNKS = (2, 2)
CALLS = ((0, 0, 2), (1, 0, 2))
DIRECT_IN = ()
DIRECT_OUT = (1,)
STEPS = ("kv0", "kv1", "z0", "q0", "q1", "z1", "att0", "o0", "r0", "dx0", "att1", "o1", "dx1", "r1")
GATES = {
    "pack": ("kv0",),
    "q1": ("q0",),
    "r11": ("o0",),
    "r21": ("o1", "dx1"),
}
SOFTCAP = 50.0
TANH_SCALE = 1.0 / (12.0 * SOFTCAP)
EXP2_SCALE = SOFTCAP * math.log2(math.e)
SCORE_SCALE = 1.0 / 12.0
F32 = jnp.float32
BF16 = jnp.bfloat16
BUFFERS = 2
JOIN = 3


def dot(a, b, ca, cb):
    return lax.dot_general(a, b, (((ca,), (cb,)), ((), ())), preferred_element_type=F32)


def vmem():
    return pl.BlockSpec(memory_space=pltpu.VMEM)


def smem():
    return pl.BlockSpec(memory_space=pltpu.SMEM)


def head_cols(index):
    return pl.ds(pl.multiple_of(index * HEAD, HEAD), HEAD)


def pack_kernel(chunks, members, group, heads_dev, info, a_ref, b_ref, *outs):
    me = info[0]
    first = 0
    for c, heads in enumerate(chunks):
        for m in range(members):
            out = outs[c * members + m]
            base = (me ^ m) * heads_dev + first
            for h in range(heads):
                for g in range(group):
                    source = head_cols((base + h) * group + g)
                    out[:, (2 * h * group + g) * HEAD : (2 * h * group + g + 1) * HEAD] = a_ref[:, source]
                    out[:, ((2 * h + 1) * group + g) * HEAD : ((2 * h + 1) * group + g + 1) * HEAD] = b_ref[:, source]
        first += heads


def pack(info, a, b, chunks, members, group, heads_dev):
    rows = a.shape[0]
    return pl.pallas_call(
        functools.partial(pack_kernel, chunks, members, group, heads_dev),
        out_shape=[
            jax.ShapeDtypeStruct((rows, 2 * h * group * HEAD), BF16) for h in chunks for _ in range(members)
        ],
        in_specs=[smem(), vmem(), vmem()],
        out_specs=[vmem()] * (len(chunks) * members),
        compiler_params=pltpu.CompilerParams(vmem_limit_bytes=40 * 2**20),
        name="pack",
    )(info, a, b)


def unpack_kernel(chunks, members, group, heads_dev, later, info, *refs):
    me = info[0]
    count = len(chunks) * members
    ins, more, (a_ref, b_ref) = refs[:count], dict(zip(later, refs[count:-2])), refs[-2:]
    first = 0
    for c, heads in enumerate(chunks):
        for m in range(members):
            at = c * members + m
            base = (me ^ m) * heads_dev + first

            def block(column):
                part = slice(column * HEAD, (column + 1) * HEAD)
                if at not in more:
                    return ins[at][:, part]
                return (ins[at][:, part].astype(F32) + more[at][:, part].astype(F32)).astype(BF16)

            for h in range(heads):
                for g in range(group):
                    target = head_cols((base + h) * group + g)
                    a_ref[:, target] = block(2 * h * group + g)
                    b_ref[:, target] = block((2 * h + 1) * group + g)
        first += heads


def unpack(info, pieces, later, chunks, members, group, heads_dev):
    rows = pieces[0].shape[0]
    width = members * heads_dev * group * HEAD
    where = tuple(later)
    more = [later[at] for at in where]
    return pl.pallas_call(
        functools.partial(unpack_kernel, chunks, members, group, heads_dev, where),
        out_shape=[jax.ShapeDtypeStruct((rows, width), BF16)] * 2,
        in_specs=[smem()] + [vmem()] * (len(pieces) + len(more)),
        out_specs=[vmem()] * 2,
        compiler_params=pltpu.CompilerParams(vmem_limit_bytes=40 * 2**20),
        name="unpack",
    )(info, *pieces, *more)


def attention_kernel(members, hops, group, rows, heads, info, *refs):
    planes = hops + 1
    kv_refs = refs[:planes]
    q_refs = refs[planes : planes + members]
    o_refs = refs[planes + members : planes + 2 * members]
    dkv_refs = refs[planes + 2 * members : 2 * planes + 2 * members]
    k_all, v_all, kt_all, vt_all, dk_all, dv_all, q_s, o_s, p_all, eg_all, ds_all = refs[2 * planes + 2 * members :]
    me = info[0]
    plane = info[1]
    blocks = WINDOW // rows + 1
    wide = group * rows
    wide_q = 2 * group * HEAD
    key_at = lax.broadcasted_iota(jnp.int32, (rows, wide), 0)
    query_at = lax.broadcasted_iota(jnp.int32, (rows, wide), 1) % rows
    behind = key_at > query_at
    seen = [(plane >= hops - k).astype(F32) for k in range(planes)]
    pairs = [(b, min(b + JOIN, blocks)) for b in range(0, blocks, JOIN)]
    state = {}

    def prepare(h):
        k_s, v_s, kt_s, vt_s = k_all.at[h % BUFFERS], v_all.at[h % BUFFERS], kt_all.at[h % BUFFERS], vt_all.at[h % BUFFERS]
        for m in range(members):
            q_s[h, m] = q_refs[m][:, h * wide_q : (h + 1) * wide_q]
        for k in range(planes):
            for s in range(members):
                at = (k * members + s) * rows
                keys = kv_refs[k][me ^ s, :, 2 * h * HEAD : (2 * h + 1) * HEAD]
                values = kv_refs[k][me ^ s, :, (2 * h + 1) * HEAD : (2 * h + 2) * HEAD]
                k_s[at : at + rows, :] = keys
                v_s[at : at + rows, :] = values
                kt_s[:, at : at + rows] = keys.T
                vt_s[:, at : at + rows] = values.T
            yield

    def forward(h, s):
        turn = (h * members + s) % BUFFERS
        k_s, vt_s = k_all.at[h % BUFFERS], vt_all.at[h % BUFFERS]
        p_s, eg_s = p_all.at[turn], eg_all.at[turn]
        q_all = q_s[h, me ^ s]
        q = jnp.concatenate([q_all[:, g * HEAD : (g + 1) * HEAD] for g in range(group)], axis=0)
        go = jnp.concatenate([q_all[:, (group + g) * HEAD : (group + g + 1) * HEAD] for g in range(group)], axis=0)
        totals = [jnp.zeros((8, wide), F32) for _ in range(planes)]
        for low, high in pairs:
            scores = dot(k_s[(s + low) * rows : (s + high) * rows, :], q, 1, 1)
            for b in range(low, high):
                score = scores[(b - low) * rows : (b - low + 1) * rows]
                t = jnp.tanh(score * TANH_SCALE)
                e = jnp.exp2(t * EXP2_SCALE)
                if b == 0:
                    e = jnp.where(behind, e, 0.0)
                if b == blocks - 1:
                    e = jnp.where(behind, 0.0, e)
                k = (s + b) // members
                totals[k] = totals[k] + jnp.sum(e.reshape(rows // 8, 8, wide), axis=0)
                p_s[b * rows : (b + 1) * rows, :] = e.astype(BF16)
                eg_s[b * rows : (b + 1) * rows, :] = e * (1.0 - t * t)
            yield
        total = sum(jnp.sum(totals[k], axis=0, keepdims=True) * seen[k] for k in range(planes))
        inverse = 1.0 / total
        got = (go.astype(F32).T * inverse).astype(BF16)
        ot = dot(vt_s[:, s * rows : (s + blocks) * rows], p_s[...], 1, 0)
        ot = (ot * inverse).astype(BF16)
        gdot = jnp.sum(ot.astype(F32) * got.astype(F32), axis=0, keepdims=True)
        o = ot.astype(F32).T.astype(BF16)
        for g in range(group):
            o_s[h, me ^ s, :, g * HEAD : (g + 1) * HEAD] = o[g * rows : (g + 1) * rows]
        state[h, s] = (q, got, gdot)
        yield

    def inner(h, s):
        turn = (h * members + s) % BUFFERS
        v_s, eg_s, ds_s = v_all.at[h % BUFFERS], eg_all.at[turn], ds_all.at[turn]
        q, got, gdot = state[h, s]
        for low, high in pairs:
            dps = dot(v_s[(s + low) * rows : (s + high) * rows, :], got, 1, 0)
            part = slice(low * rows, high * rows)
            ds_s[part, :] = ((dps - gdot) * eg_s[part, :]).astype(BF16)
            yield

    def outer(h, s):
        turn = (h * members + s) % BUFFERS
        kt_s, dk_s, dv_s = kt_all.at[h % BUFFERS], dk_all.at[h % BUFFERS], dv_all.at[h % BUFFERS]
        p_s, ds_s = p_all.at[turn], ds_all.at[turn]
        q, got, gdot = state.pop((h, s))
        old = slice(s * rows, (s + blocks - 1) * rows)
        new = slice((s + blocks - 1) * rows, (s + blocks) * rows)

        def add(into, value):
            if s:
                into[old, :] += value[: (blocks - 1) * rows]
                into[new, :] = value[(blocks - 1) * rows :]
            else:
                into[: blocks * rows, :] = value

        add(dv_s, dot(p_s[...], got, 1, 1))
        yield
        add(dk_s, dot(ds_s[...], q, 1, 0))
        yield
        dqt = dot(kt_s[:, s * rows : (s + blocks) * rows], ds_s[...], 1, 0)
        dq = (dqt * SCORE_SCALE).T.astype(BF16)
        for g in range(group):
            o_s[h, me ^ s, :, (group + g) * HEAD : (group + g + 1) * HEAD] = dq[g * rows : (g + 1) * rows]
        yield

    def finish(h):
        dk_s, dv_s = dk_all.at[h % BUFFERS], dv_all.at[h % BUFFERS]
        for k in range(planes):
            for s in range(members):
                at = (k * members + s) * rows
                keys = (dk_s[at : at + rows, :] * SCORE_SCALE).astype(BF16)
                dkv_refs[k][me ^ s, :, 2 * h * HEAD : (2 * h + 1) * HEAD] = keys
                dkv_refs[k][me ^ s, :, (2 * h + 1) * HEAD : (2 * h + 2) * HEAD] = dv_s[at : at + rows, :].astype(BF16)
            yield
        for m in range(members):
            o_refs[m][:, h * wide_q : (h + 1) * wide_q] = o_s[h, m]

    def together(*walks):
        walks = list(walks)
        while walks:
            for walk in list(walks):
                if next(walk, walk) is walk:
                    walks.remove(walk)

    tiles = [(h, s) for h in range(heads) for s in range(members)]
    together(prepare(0))
    together(forward(0, 0))
    for i, (h, s) in enumerate(tiles):
        together(inner(h, s))
        beside = [outer(h, s)]
        if i + 1 < len(tiles):
            beside.insert(0, forward(*tiles[i + 1]))
        if s == 1 and h + 1 < heads:
            beside.append(prepare(h + 1))
        if s == 0 and h > 0:
            beside.append(finish(h - 1))
        together(*beside)
    together(finish(heads - 1))


def attention(info, kvs, qs, group, first=0, heads=None):
    planes, members = len(kvs), len(qs)
    rows = qs[0].shape[0]
    heads = kvs[0].shape[2] // (2 * HEAD)
    keys_all = planes * members * rows
    wide = group * rows
    span = WINDOW + rows
    return pl.pallas_call(
        functools.partial(attention_kernel, members, planes - 1, group, rows, heads),
        out_shape=[jax.ShapeDtypeStruct(q.shape, BF16) for q in qs]
        + [jax.ShapeDtypeStruct(kv.shape, BF16) for kv in kvs],
        in_specs=[smem()] + [vmem()] * (planes + members),
        out_specs=[vmem()] * (planes + members),
        scratch_shapes=[
            pltpu.VMEM((BUFFERS, keys_all, HEAD), BF16),
            pltpu.VMEM((BUFFERS, keys_all, HEAD), BF16),
            pltpu.VMEM((BUFFERS, HEAD, keys_all), BF16),
            pltpu.VMEM((BUFFERS, HEAD, keys_all), BF16),
            pltpu.VMEM((BUFFERS, keys_all, HEAD), F32),
            pltpu.VMEM((BUFFERS, keys_all, HEAD), F32),
            pltpu.VMEM((heads, members, rows, 2 * group * HEAD), BF16),
            pltpu.VMEM((heads, members, rows, 2 * group * HEAD), BF16),
            pltpu.VMEM((BUFFERS, span, wide), BF16),
            pltpu.VMEM((BUFFERS, span, wide), F32),
            pltpu.VMEM((BUFFERS, span, wide), BF16),
        ],
        compiler_params=pltpu.CompilerParams(vmem_limit_bytes=40 * 2**20),
        cost_estimate=pl.CostEstimate(
            flops=12 * heads * members * wide * span * HEAD,
            bytes_accessed=2 * heads * members * rows * 4 * HEAD * (planes + group),
            transcendentals=2 * heads * members * wide * span,
        ),
        name="attention",
    )(info, *kvs, *qs)


def after(value, *earlier):
    leaves = [leaf for leaf in jax.tree.leaves(earlier)]
    return lax.optimization_barrier((value, leaves))[0] if leaves else value


def on_device(queries, keys, values, output_gradient):
    rows = queries.shape[0]
    tp = lax.axis_size("tp")
    ctx = lax.axis_size("ctx")
    members = INNER * tp
    heads_dev = keys.shape[1] // HEAD // members
    group = queries.shape[1] // keys.shape[1]
    hops = max(1, WINDOW // (members * rows))
    device = lax.axis_index("ctx") * tp + lax.axis_index("tp")
    info = jnp.stack([device % members, device // members]).astype(jnp.int32)
    axes = ("ctx", "tp")

    def swap(pieces):
        pairs = [[(i, i ^ m) for i in range(ctx * tp)] for m in range(members)]
        return [pieces[0]] + [lax.ppermute(pieces[m], axes, pairs[m]) for m in range(1, members)]

    def hop(array, by):
        pairs = [(i, i + by * members) for i in range(ctx * tp) if 0 <= i + by * members < ctx * tp]
        return lax.ppermute(array, axes, pairs)

    def hop_across(pieces, by):
        count = ctx * tp
        pairs = [
            [(i, (i ^ m) + by * members) for i in range(count) if 0 <= (i ^ m) + by * members < count]
            for m in range(members)
        ]
        return [lax.ppermute(pieces[m], axes, pairs[m]) for m in range(members)]

    kv_packed = pack(info, keys, values, CHUNKS, members, 1, heads_dev)
    done = {}
    q_packed = []

    def gated(value, step):
        earlier = [done[name] for name in GATES.get(step, ()) if name in done]
        return after(value, *earlier)

    def run(step):
        kind, c = step[:-1], int(step[-1])
        if kind == "kv":
            done[step] = swap(gated(kv_packed[c * members : (c + 1) * members], step))
        elif kind == "q":
            if not q_packed:
                q_packed.extend(
                    pack(info, gated(queries, "pack"), output_gradient, CHUNKS, members, group, heads_dev)
                )
            done[step] = swap(gated(q_packed[c * members : (c + 1) * members], step))
        elif kind.startswith("z"):
            k = int(kind[1:])
            if k == 1 and c in DIRECT_IN:
                pieces = hop_across(gated(kv_packed[c * members : (c + 1) * members], step), 1)
                done[f"first{c}"] = pieces[0]
                done[step] = jnp.stack(pieces)
            else:
                if k == 1:
                    done[f"z0{c}"] = jnp.stack(done[f"kv{c}"])
                done[step] = hop(gated(done[f"z{k - 1}{c}"], step), 1)
        elif kind == "att":
            part, first, heads = CALLS[c]
            if f"z0{part}" not in done:
                done[f"z0{part}"] = jnp.stack(done[f"kv{part}"])
            halo = [done[f"z{k}{part}"] for k in range(hops, -1, -1)]
            halo, pieces = gated((halo, done[f"q{part}"]), step)
            results = attention(info, halo, pieces, group, first, heads)
            done[step] = results[members:]
            done[f"os{c}"] = results[:members]
            done[f"r0{c}"] = results[members]
        elif kind == "o":
            done[step] = swap(gated(done[f"os{c}"], step))
        elif kind.startswith("r"):
            k = int(kind[1:])
            carried = gated(done[f"r{k - 1}{c}"], step)
            if k == hops and c in DIRECT_OUT:
                done[step] = hop_across([carried[m] for m in range(members)], -1)
                return
            arrived = hop(carried, -1)
            done[step] = (arrived.astype(F32) + done[f"att{c}"][k].astype(F32)).astype(BF16)
        else:
            carried = gated(done[f"att{c}"][hops] if c in DIRECT_OUT else done[f"r{hops}{c}"], step)
            done[step] = swap([carried[m] for m in range(members)])

    for step in STEPS:
        kind = step[:-1]
        if kind in ("z", "r"):
            for k in range(1, hops + 1):
                run(f"{kind}{k}{step[-1]}")
        else:
            run(step)
    returned = [heads for _, _, heads in CALLS]
    o_all = sum([done[f"o{c}"] for c in range(len(CALLS))], [])
    dkv_all = sum([done[f"dx{c}"] for c in range(len(CALLS))], [])
    attended, query_grad = unpack(info, o_all, {}, returned, members, group, heads_dev)
    later = {c * members + m: done[f"r{hops}{c}"][m] for c in DIRECT_OUT for m in range(members)}
    key_grad, value_grad = unpack(info, dkv_all, later, returned, members, 1, heads_dev)
    return attended, query_grad, key_grad, value_grad


def solution(mesh):
    placed = P(("group", "ctx", "tp"), None)
    return jax.shard_map(
        on_device, mesh=mesh, in_specs=(placed,) * 4, out_specs=(placed,) * 4, check_vma=False
    )
```
